32 devices in a mesh: gx: 4 (over y, x), gy: 8 (over z, core).
Axes of the slice: x: 2, y: 2, z: 4, core: 2. Of those that a mesh axis runs over, the one named last changes fastest.
Arguments:
- labels: float32 [131072, 256], P(('gx', 'gy')), may hold values from 0 to 24, as said below
- weights: bfloat16 [1024, 12, 128, 128], P(('gx', 'gy')), may hold values from 0.001 to 1, as said below
- column_index: int32 [1024, 12], P(('gx', 'gy')), may hold values from 0 to 47, as said below
- send_index: int32 [32, 4, 4], P(('gx', 'gy')), may hold values from 0 to 31, as said below
- seed_doc: int32 [8192], P(('gx', 'gy')), may hold values from 0 to 4095
- seed_topic: int32 [8192], P(('gx', 'gy')), may hold values from 0 to 255
Outputs:
- spread: float32 [131072, 256], P(('gx', 'gy'))
The draws below stay inside these ranges and needn't reach their ends.
Inputs may be any that keep to these rules, and one draw needn't show every extreme that they name: `column_index`: slot 0 of a row block names the row block itself (its index within the partition). A value below 32 names a block of the partition's own labels; 32 + d * 4 + s names slot s of what neighbour d hands over; only existing neighbours are named, and only in the last 3 slots. `send_index`: the 4 entries of one partition and direction are distinct. `weights`: entries are positive. `labels`: entries are nonnegative.
All inputs are finite; a program needn't handle non-finite values.
Results may differ from the reference program's by a relative error of at most 0.0004.
Values may be sent and summed in bfloat16 or wider, within the bound.
No kernel may reach another device: no remote copies, remote signals or barrier semaphores. Data moves between devices by JAX's collectives and lax.ppermute only.
A program may use at most 128 MiB of HBM per device.

```python
import math
import jax
import jax.numpy as jnp
from jax import lax

TOPICS = 256
BLOCK = 128
SLOTS = 12
REMOTE = 3
SENDS = 4
ITERS = 2
BLOCKS_DEV = 32
SEED_DEV = 256
DOCS_DEV = 4096
DOCS = 131072
ROW_BLOCKS = 1024
SEEDS = 8192
N_GX = 4
N_GY = 8
DEVICES = 32


def draw_labels(key, part):
    first_key, second_key, third_key = jax.random.split(key, 3)
    block_level = jnp.exp(jax.random.uniform(first_key, (ROW_BLOCKS, 1, 1), jnp.float32, math.log(0.5), math.log(4.0)))
    topic_level = jnp.exp(jax.random.uniform(second_key, (1, 1, TOPICS), jnp.float32, math.log(0.5), math.log(6.0)))
    rough = jax.random.uniform(third_key, (ROW_BLOCKS, BLOCK, TOPICS), jnp.float32, 0.0, 1.0)
    values = block_level * topic_level * rough
    values = values.reshape(DOCS, TOPICS)
    top = jnp.max(values)
    return (values / top * 24.0).astype(jnp.float32)


def draw_weights(key, part):
    total = BLOCKS_DEV * DEVICES
    logs = jax.random.uniform(key, (total, SLOTS, BLOCK, BLOCK), jnp.float32, math.log(0.001), 0.0)
    values = jnp.exp(logs)
    return values.astype(jnp.bfloat16)


def draw_column_index(key, part):
    total = BLOCKS_DEV * DEVICES
    first_key, second_key, third_key = jax.random.split(key, 3)
    rows = jnp.arange(total, dtype=jnp.int32)
    device = rows // BLOCKS_DEV
    local = rows % BLOCKS_DEV
    outer = device // N_GY
    inner = device % N_GY
    local_cols = jax.random.randint(first_key, (total, SLOTS - REMOTE - 1), 0, BLOCKS_DEV, dtype=jnp.int32)
    offsets = jax.random.randint(second_key, (DEVICES,), 0, 4, dtype=jnp.int32)[device]
    position = local[:, None] * REMOTE + jnp.arange(REMOTE, dtype=jnp.int32)[None, :]
    direction = (position + offsets[:, None]) % 4
    present = jnp.where(direction == 0, inner[:, None] > 0, jnp.where(direction == 1, inner[:, None] < N_GY - 1, jnp.where(direction == 2, outer[:, None] > 0, outer[:, None] < N_GX - 1)))
    flipped = direction // 2 * 2 + 1 - direction % 2
    direction = jnp.where(present, direction, flipped)
    slot = jax.random.randint(third_key, (total, REMOTE), 0, SENDS, dtype=jnp.int32)
    remote = BLOCKS_DEV + direction * SENDS + slot
    return jnp.concatenate([local[:, None], local_cols, remote], axis=1).astype(jnp.int32)


def pick_blocks(subkey):
    return jax.random.permutation(subkey, BLOCKS_DEV)[:SENDS]


def draw_send_index(key, part):
    keys = jax.random.split(key, DEVICES * 4)
    chosen = jax.vmap(pick_blocks)(keys)
    return chosen.reshape(DEVICES, 4, SENDS).astype(jnp.int32)


def with_ends(drawn, key, low, top_value):
    extent = drawn.shape
    place = [jax.random.randint(jax.random.fold_in(key, axis), (), 0, extent[axis]) for axis in range(len(extent))]
    drawn = drawn.at[tuple(place)].set(low)
    longest = extent.index(max(extent))
    place[longest] = (place[longest] + 1) % extent[longest]
    return drawn.at[tuple(place)].set(top_value)


def setup_inputs(seed: int = 0) -> dict:
    streams_of = jax.random.split(jax.random.key(seed), 7)
    return {
        "labels": draw_labels(jax.random.fold_in(streams_of[6], 71), 0),
        "weights": draw_weights(jax.random.fold_in(streams_of[6], 71), 0),
        "column_index": draw_column_index(jax.random.fold_in(streams_of[6], 71), 0),
        "send_index": draw_send_index(jax.random.fold_in(streams_of[6], 71), 0),
        "seed_doc": with_ends(jax.random.randint(streams_of[4], (SEEDS,), 0, DOCS_DEV), jax.random.fold_in(streams_of[4], 1), 0, DOCS_DEV - 1).astype(jnp.int32),
        "seed_topic": with_ends(jax.random.randint(streams_of[5], (SEEDS,), 0, TOPICS), jax.random.fold_in(streams_of[5], 1), 0, TOPICS - 1).astype(jnp.int32),
    }


ALPHA = 0.99
GAIN = 1.0 / (1.0 - 0.99)

def shift_forward(values, axis):
    first = jnp.zeros_like(lax.slice_in_dim(values, 0, 1, axis=axis))
    rest = lax.slice_in_dim(values, 0, values.shape[axis] - 1, axis=axis)
    return jnp.concatenate([first, rest], axis=axis)

def shift_backward(values, axis):
    last = jnp.zeros_like(lax.slice_in_dim(values, 0, 1, axis=axis))
    rest = lax.slice_in_dim(values, 1, values.shape[axis], axis=axis)
    return jnp.concatenate([rest, last], axis=axis)

def degree_of(weight_part):
    return lax.optimization_barrier(jnp.sum(weight_part.astype(jnp.float32), axis=(1, 3)))

def select_sent(scaled_part, index_part):
    return scaled_part[index_part]

def block_products(items):
    weight_part, extended_part, column_part = items
    picked = extended_part[column_part]
    return jnp.einsum('rkij,rkjc->ric', weight_part.astype(jnp.float32), picked.astype(jnp.float32))

def reference(labels, weights, column_index, send_index, seed_doc, seed_topic):
    per_device = weights.reshape(DEVICES, BLOCKS_DEV, SLOTS, BLOCK, BLOCK)
    degree = lax.map(degree_of, per_device)
    scale = (1.0 / jnp.sqrt(degree)).reshape(DOCS, 1)
    owners = jnp.arange(SEEDS, dtype=jnp.int32) // SEED_DEV
    rows = owners * DOCS_DEV + seed_doc
    seeds = jnp.zeros((DOCS, TOPICS), jnp.float32).at[rows, seed_topic].add(GAIN)
    columns = column_index.reshape(DEVICES, BLOCKS_DEV, SLOTS)
    current = labels
    for iteration in range(ITERS):
        scaled = (scale * current).astype(jnp.bfloat16).reshape(DEVICES, BLOCKS_DEV, BLOCK, TOPICS)
        sent = jax.vmap(select_sent)(scaled, send_index)
        sent = sent.reshape(N_GX, N_GY, 4, SENDS, BLOCK, TOPICS)
        from_lower_inner = shift_forward(sent[:, :, 1], 1)
        from_upper_inner = shift_backward(sent[:, :, 0], 1)
        from_lower_outer = shift_forward(sent[:, :, 3], 0)
        from_upper_outer = shift_backward(sent[:, :, 2], 0)
        received = jnp.stack([from_lower_inner, from_upper_inner, from_lower_outer, from_upper_outer], axis=2)
        received = received.reshape(DEVICES, 4 * SENDS, BLOCK, TOPICS)
        extended = jnp.concatenate([scaled, received], axis=1)
        product = lax.map(block_products, (per_device, extended, columns))
        product = product.reshape(DOCS, TOPICS)
        current = ALPHA * scale * product + (1.0 - ALPHA) * seeds
    return current
```

```python
import functools

import jax
import jax.numpy as jnp
from jax import lax
from jax.experimental import pallas as pl
from jax.experimental.pallas import tpu as pltpu
from jax.sharding import PartitionSpec as P

ITERS = 2

ALPHA = 0.99
GAIN = 1.0 / (1.0 - 0.99)
SEED_WEIGHT = (1.0 - ALPHA) * GAIN

LOCAL = 8
VMEM = pltpu.VMEM
IN_VMEM = pl.BlockSpec(memory_space=pltpu.VMEM)
IN_SMEM = pl.BlockSpec(memory_space=pltpu.SMEM)
ANYWHERE = pl.BlockSpec(memory_space=pl.ANY)


def call(body, out_shape, out_specs, in_specs, scratch=(), aliases=None, limit=8):
    return pl.pallas_call(
        body,
        out_shape=out_shape,
        in_specs=in_specs,
        out_specs=out_specs,
        scratch_shapes=scratch,
        input_output_aliases=aliases or {},
        compiler_params=pltpu.CompilerParams(vmem_limit_bytes=limit * 2**20),
        cost_estimate=pl.CostEstimate(flops=1, bytes_accessed=1, transcendentals=0),
    )


def pinned(value):
    return pltpu.with_memory_space_constraint(value, pltpu.VMEM)


def unmoved(value):
    return pltpu.with_memory_space_constraint(value, pltpu.HBM)


def row_scale(weights, row):
    slots = weights.shape[1]
    total = weights[row, 0].astype(jnp.float32)
    for slot in range(1, slots):
        total = total + weights[row, slot].astype(jnp.float32)
    return lax.rsqrt(jnp.sum(total, axis=1, keepdims=True))


def spread_over(scale, width):
    return jnp.concatenate([scale] * (width // scale.shape[1]), axis=1)


def toward_x(odd):
    turn = odd[0]
    return (3 - turn, 2 + turn)


def toward_y(odd):
    turn = odd[0]
    return (1 - turn, turn)


def sent_row(send_index, order, sends, i):
    return send_index[0, order[i // sends], i % sends]


def weighted(weights, extended, columns, row, first, last):
    left = jnp.concatenate([weights[row, slot] for slot in range(first, last)], axis=1)
    right = jnp.concatenate([extended[columns[slot, row]] for slot in range(first, last)], axis=0)
    return jnp.dot(left, right, preferred_element_type=jnp.float32)


def first_send_body(send_index, odd_x, weights, labels, out_a, out_b, held, block, sem):
    sends = out_a.shape[0]
    order = toward_x(odd_x)

    def copies(i):
        row = sent_row(send_index, order, sends, i)
        return (
            pltpu.make_async_copy(weights.at[row], held.at[i], sem.at[i, 0]),
            pltpu.make_async_copy(labels.at[row], block.at[i], sem.at[i, 1]),
        )

    for i in range(2 * sends):
        for copy in copies(i):
            copy.start()
    for i in range(2 * sends):
        for copy in copies(i):
            copy.wait()
        out = out_a if i < sends else out_b
        out[i % sends] = (row_scale(held, i) * block[i]).astype(jnp.bfloat16)


def degree_body(send_index, odd_y, weights, labels, held, extended, scales, out_a, out_b, block, sem, *, chunk):
    blocks_dev = weights.shape[0]
    sends = out_a.shape[0]
    chunks = blocks_dev // chunk

    def copies(c):
        part = pl.ds(c * chunk, chunk)
        return (
            pltpu.make_async_copy(weights.at[part], held.at[part], sem.at[c, 0]),
            pltpu.make_async_copy(labels.at[part], block.at[part], sem.at[c, 1]),
        )

    for c in range(chunks):
        for copy in copies(c):
            copy.start()

    def step(c, carry):
        for copy in copies(c):
            copy.wait()
        for i in range(chunk):
            row = c * chunk + i
            scale = row_scale(held, row)
            scales[row] = jnp.broadcast_to(scale, scales.shape[1:])
            extended[row] = (scale * block[row]).astype(jnp.bfloat16)
        return carry

    lax.fori_loop(0, chunks, step, 0)
    order = toward_y(odd_y)
    for i in range(sends):
        out_a[i] = extended[sent_row(send_index, order, sends, i)]
        out_b[i] = extended[sent_row(send_index, order, sends, sends + i)]


def local_body(columns, seed_doc, seed_topic, weights, extended, scales, out, topic_hot, *, unroll):
    blocks_dev, block_size, topics = out.shape
    seeds = seed_doc.shape[1]
    topic = lax.broadcasted_iota(jnp.int32, (topics, seeds), 0)
    hot = jnp.where(topic == seed_topic[...], 1.0, 0.0).astype(jnp.float32)
    topic_hot[...] = hot.T.astype(jnp.bfloat16)

    def step(row, carry):
        product = weighted(weights, extended, columns, row, 0, LOCAL)
        document = lax.broadcasted_iota(jnp.int32, (block_size, seeds), 0) + row * block_size
        doc_hot = jnp.where(document == seed_doc[...], 1.0, 0.0).astype(jnp.bfloat16)
        counts = jnp.dot(doc_hot, topic_hot[...], preferred_element_type=jnp.float32)
        factor = spread_over(ALPHA * scales[row], topics)
        out[row] = factor * product + SEED_WEIGHT * counts
        return carry

    lax.fori_loop(0, blocks_dev, step, 0, unroll=unroll)


def arrivals(received, extended, odd_x, odd_y, sem):
    sends = received[0].shape[0]
    low = extended.shape[0] - 4 * sends
    order = toward_x(odd_x) + toward_y(odd_y)
    copies = [
        pltpu.make_async_copy(value, extended.at[pl.ds(low + order[i] * sends, sends)], sem.at[i])
        for i, value in enumerate(received)
    ]
    for copy in copies:
        copy.start()
    for copy in copies:
        copy.wait()


def finished(weights, extended, columns, scales, partial, row):
    topics = partial.shape[2]
    slots = weights.shape[1]
    product = weighted(weights, extended, columns, row, LOCAL, slots)
    return partial[row] + spread_over(ALPHA * scales[row], topics) * product


def second_send_body(
    columns, send_index, odd_x, odd_y, weights, extended_in, scales, partial, r0, r1, r2, r3, out_a, out_b, extended, sem
):
    sends = out_a.shape[0]
    topics = out_a.shape[2]
    arrivals((r0, r1, r2, r3), extended, odd_x, odd_y, sem)
    order = toward_x(odd_x)
    for i in range(2 * sends):
        row = sent_row(send_index, order, sends, i)
        value = finished(weights, extended, columns, scales, partial, row)
        out = out_a if i < sends else out_b
        out[i % sends] = (spread_over(scales[row], topics) * value).astype(jnp.bfloat16)


def rest_body(columns, send_index, odd_y, weights, extended, scales, partial, following, out_a, out_b, *, unroll):
    blocks_dev, _, topics = partial.shape
    sends = out_a.shape[0]

    def step(row, carry):
        value = finished(weights, extended, columns, scales, partial, row)
        following[row] = (spread_over(scales[row], topics) * value).astype(jnp.bfloat16)
        return carry

    lax.fori_loop(0, blocks_dev, step, 0, unroll=unroll)
    order = toward_y(odd_y)
    for i in range(sends):
        out_a[i] = following[sent_row(send_index, order, sends, i)]
        out_b[i] = following[sent_row(send_index, order, sends, sends + i)]


def last_body(
    columns, odd_x, odd_y, weights, extended_in, scales, partial, r0, r1, r2, r3, out, extended, block, sem, out_sem, *, chunk
):
    blocks_dev = partial.shape[0]
    chunks = blocks_dev // chunk
    arrivals((r0, r1, r2, r3), extended, odd_x, odd_y, sem)

    def leave(c):
        part = pl.ds(c * chunk, chunk)
        return pltpu.make_async_copy(block.at[part], out.at[part], out_sem.at[c])

    def step(c, carry):
        for i in range(chunk):
            row = c * chunk + i
            block[row] = finished(weights, extended, columns, scales, partial, row)
        leave(c).start()
        return carry

    lax.fori_loop(0, chunks, step, 0)
    for c in range(chunks):
        leave(c).wait()


def swapped(value, axis, first):
    count = lax.axis_size(axis)
    pairs = []
    for low in range(first, count - 1, 2):
        pairs += [(low, low + 1), (low + 1, low)]
    return lax.ppermute(value, axis, pairs)


def local(labels, weights, column_index, send_index, seed_doc, seed_topic):
    blocks_dev, slots, block_size, _ = weights.shape
    documents = blocks_dev * block_size
    topics = labels.shape[1]
    sends = send_index.shape[2]
    seeds = seed_doc.shape[0]
    chunk = 4
    labels = unmoved(labels.reshape(blocks_dev, block_size, topics))
    weights = unmoved(weights)
    seed_doc = seed_doc.reshape(1, seeds)
    seed_topic = seed_topic.reshape(1, seeds)
    columns = column_index.T
    odd_x = (lax.axis_index("gx") % 2).reshape(1)
    odd_y = (lax.axis_index("gy") % 2).reshape(1)

    sent = VMEM((sends, block_size, topics), jnp.bfloat16)
    extended_shape = VMEM((blocks_dev + 4 * sends, block_size, topics), jnp.bfloat16)
    partial_shape = VMEM((blocks_dev, block_size, topics), jnp.float32)

    xa, xb = call(
        first_send_body,
        (sent, sent),
        (IN_VMEM, IN_VMEM),
        (IN_SMEM, IN_SMEM, ANYWHERE, ANYWHERE),
        (
            pltpu.VMEM((2 * sends, slots, block_size, block_size), jnp.bfloat16),
            pltpu.VMEM((2 * sends, block_size, topics), jnp.float32),
            pltpu.SemaphoreType.DMA((2 * sends, 2)),
        ),
    )(send_index, odd_x, weights, labels)
    xa, xb = swapped(xa, "gx", 0), swapped(xb, "gx", 1)

    held, extended, scales, ya, yb = call(
        functools.partial(degree_body, chunk=chunk),
        (
            VMEM(weights.shape, jnp.bfloat16),
            extended_shape,
            VMEM((blocks_dev, block_size, block_size), jnp.float32),
            sent,
            sent,
        ),
        (IN_VMEM,) * 5,
        (IN_SMEM, IN_SMEM, ANYWHERE, ANYWHERE),
        (
            pltpu.VMEM((blocks_dev, block_size, topics), jnp.float32),
            pltpu.SemaphoreType.DMA((blocks_dev // chunk, 2)),
        ),
    )(send_index, odd_y, weights, labels)
    ya, yb = swapped(ya, "gy", 0), swapped(yb, "gy", 1)

    def near(extended):
        return call(
            functools.partial(local_body, unroll=4),
            partial_shape,
            IN_VMEM,
            (IN_SMEM, IN_VMEM, IN_VMEM, IN_VMEM, IN_VMEM, IN_VMEM),
            (pltpu.VMEM((seeds, topics), jnp.bfloat16),),
        )(columns, seed_doc, seed_topic, pinned(held), pinned(extended), pinned(scales))

    partial = near(extended)
    xa, xb, extended = call(
        second_send_body,
        (sent, sent, extended_shape),
        (IN_VMEM,) * 3,
        (IN_SMEM,) * 4 + (IN_VMEM,) * 4 + (ANYWHERE,) * 4,
        (pltpu.SemaphoreType.DMA((4,)),),
        aliases={5: 2},
    )(columns, send_index, odd_x, odd_y, pinned(held), pinned(extended), pinned(scales), pinned(partial), xa, xb, ya, yb)
    xa, xb = swapped(xa, "gx", 0), swapped(xb, "gx", 1)

    following, ya, yb = call(
        functools.partial(rest_body, unroll=4),
        (extended_shape, sent, sent),
        (IN_VMEM,) * 3,
        (IN_SMEM,) * 3 + (IN_VMEM,) * 4,
    )(columns, send_index, odd_y, pinned(held), pinned(extended), pinned(scales), pinned(partial))
    ya, yb = swapped(ya, "gy", 0), swapped(yb, "gy", 1)

    partial = near(following)
    out, _ = call(
        functools.partial(last_body, chunk=chunk),
        (jax.ShapeDtypeStruct((blocks_dev, block_size, topics), jnp.float32), extended_shape),
        (ANYWHERE, IN_VMEM),
        (IN_SMEM,) * 3 + (IN_VMEM,) * 4 + (ANYWHERE,) * 4,
        (
            pltpu.VMEM((blocks_dev, block_size, topics), jnp.float32),
            pltpu.SemaphoreType.DMA((4,)),
            pltpu.SemaphoreType.DMA((blocks_dev // chunk,)),
        ),
        aliases={4: 1},
    )(columns, odd_x, odd_y, pinned(held), pinned(following), pinned(scales), pinned(partial), xa, xb, ya, yb)
    return out.reshape(documents, topics)


def solution(mesh):
    in_specs = (
        P(("gx", "gy"), None),
        P(("gx", "gy"), None, None, None),
        P(("gx", "gy"), None),
        P(("gx", "gy"), None, None),
        P(("gx", "gy")),
        P(("gx", "gy")),
    )
    out_specs = P(("gx", "gy"), None)
    return jax.shard_map(local, mesh=mesh, in_specs=in_specs, out_specs=out_specs, check_vma=False)
```

```python
import functools

import jax
import jax.numpy as jnp
from jax import lax
from jax.experimental import pallas as pl
from jax.experimental.pallas import tpu as pltpu
from jax.sharding import PartitionSpec as P

ITERS = 2

ALPHA = 0.99
GAIN = 1.0 / (1.0 - 0.99)
SEED_WEIGHT = (1.0 - ALPHA) * GAIN

LOCAL = 8
VMEM = pltpu.VMEM
IN_VMEM = pl.BlockSpec(memory_space=pltpu.VMEM)
IN_SMEM = pl.BlockSpec(memory_space=pltpu.SMEM)
ANYWHERE = pl.BlockSpec(memory_space=pl.ANY)


def call(body, out_shape, out_specs, in_specs, scratch=(), aliases=None, limit=8):
    return pl.pallas_call(
        body,
        out_shape=out_shape,
        in_specs=in_specs,
        out_specs=out_specs,
        scratch_shapes=scratch,
        input_output_aliases=aliases or {},
        compiler_params=pltpu.CompilerParams(vmem_limit_bytes=limit * 2**20),
        cost_estimate=pl.CostEstimate(flops=1, bytes_accessed=1, transcendentals=0),
    )


def pinned(value):
    return pltpu.with_memory_space_constraint(value, pltpu.VMEM)


def unmoved(value):
    return pltpu.with_memory_space_constraint(value, pltpu.HBM)


def row_scale(weights, row):
    slots = weights.shape[1]
    total = weights[row, 0].astype(jnp.float32)
    for slot in range(1, slots):
        total = total + weights[row, slot].astype(jnp.float32)
    return lax.rsqrt(jnp.sum(total, axis=1, keepdims=True))


def spread_over(scale, width):
    return jnp.concatenate([scale] * (width // scale.shape[1]), axis=1)


def toward_x(odd):
    turn = odd[0]
    return (3 - turn, 2 + turn)


def toward_y(odd):
    turn = odd[0]
    return (1 - turn, turn)


def sent_row(send_index, order, sends, i):
    return send_index[0, order[i // sends], i % sends]


def weighted(weights, extended, columns, row, first, last):
    left = jnp.concatenate([weights[row, slot] for slot in range(first, last)], axis=1)
    right = jnp.concatenate([extended[columns[slot, row]] for slot in range(first, last)], axis=0)
    return jnp.dot(left, right, preferred_element_type=jnp.float32)


def first_send_body(send_index, odd_x, weights, labels, out_a, out_b, held, block, sem):
    sends = out_a.shape[0]
    order = toward_x(odd_x)

    def copies(i):
        row = sent_row(send_index, order, sends, i)
        return (
            pltpu.make_async_copy(weights.at[row], held.at[i], sem.at[i, 0]),
            pltpu.make_async_copy(labels.at[row], block.at[i], sem.at[i, 1]),
        )

    for i in range(2 * sends):
        for copy in copies(i):
            copy.start()
    for i in range(2 * sends):
        for copy in copies(i):
            copy.wait()
        out = out_a if i < sends else out_b
        out[i % sends] = (row_scale(held, i) * block[i]).astype(jnp.bfloat16)


def degree_body(
    send_index, odd_y, seed_doc, seed_topic, weights, labels, held, extended, scales, counts, out_a, out_b,
    block, topic_hot, sem, *, chunk,
):
    blocks_dev, block_size, topics = labels.shape
    seeds = seed_doc.shape[1]
    sends = out_a.shape[0]
    chunks = blocks_dev // chunk

    def copies(c):
        part = pl.ds(c * chunk, chunk)
        return (
            pltpu.make_async_copy(weights.at[part], held.at[part], sem.at[c, 0]),
            pltpu.make_async_copy(labels.at[part], block.at[part], sem.at[c, 1]),
        )

    for c in range(chunks):
        for copy in copies(c):
            copy.start()
    topic = lax.broadcasted_iota(jnp.int32, (topics, seeds), 0)
    hot = jnp.where(topic == seed_topic[...], 1.0, 0.0).astype(jnp.float32)
    topic_hot[...] = hot.T.astype(jnp.bfloat16)

    def step(c, carry):
        for copy in copies(c):
            copy.wait()
        for i in range(chunk):
            row = c * chunk + i
            scale = row_scale(held, row)
            scales[row] = jnp.broadcast_to(scale, scales.shape[1:])
            extended[row] = (scale * block[row]).astype(jnp.bfloat16)
            document = lax.broadcasted_iota(jnp.int32, (block_size, seeds), 0) + row * block_size
            doc_hot = jnp.where(document == seed_doc[...], 1.0, 0.0).astype(jnp.bfloat16)
            hits = jnp.dot(doc_hot, topic_hot[...], preferred_element_type=jnp.float32)
            counts[row] = hits.astype(jnp.bfloat16)
        return carry

    lax.fori_loop(0, chunks, step, 0)
    order = toward_y(odd_y)
    for i in range(sends):
        out_a[i] = extended[sent_row(send_index, order, sends, i)]
        out_b[i] = extended[sent_row(send_index, order, sends, sends + i)]


def near(weights, extended, columns, scales, counts, row):
    topics = extended.shape[2]
    product = weighted(weights, extended, columns, row, 0, LOCAL)
    return spread_over(ALPHA * scales[row], topics) * product + SEED_WEIGHT * counts[row].astype(jnp.float32)


def near_body(columns, weights, extended, scales, counts, partial, *, unroll):
    def step(row, carry):
        partial[row] = near(weights, extended, columns, scales, counts, row)
        return carry

    lax.fori_loop(0, partial.shape[0], step, 0, unroll=unroll)


def arrivals(received, extended, odd_x, odd_y, sem):
    sends = received[0].shape[0]
    low = extended.shape[0] - 4 * sends
    order = toward_x(odd_x) + toward_y(odd_y)
    copies = [
        pltpu.make_async_copy(value, extended.at[pl.ds(low + order[i] * sends, sends)], sem.at[i])
        for i, value in enumerate(received)
    ]
    for copy in copies:
        copy.start()
    for copy in copies:
        copy.wait()


def finished(weights, extended, columns, scales, partial, row):
    topics = partial.shape[2]
    slots = weights.shape[1]
    product = weighted(weights, extended, columns, row, LOCAL, slots)
    return partial[row] + spread_over(ALPHA * scales[row], topics) * product


def second_send_body(
    columns, send_index, odd_x, odd_y, weights, extended_in, scales, partial, r0, r1, r2, r3,
    x_a, x_b, y_a, y_b, extended, sem,
):
    sends = x_a.shape[0]
    topics = x_a.shape[2]
    arrivals((r0, r1, r2, r3), extended, odd_x, odd_y, sem)
    outs = (x_a, x_b, y_a, y_b)
    order = toward_x(odd_x) + toward_y(odd_y)
    for i in range(len(outs) * sends):
        row = sent_row(send_index, order, sends, i)
        value = finished(weights, extended, columns, scales, partial, row)
        outs[i // sends][i % sends] = (spread_over(scales[row], topics) * value).astype(jnp.bfloat16)


def rest_body(columns, weights, extended, scales, counts, partial, following, next_partial, *, unroll):
    blocks_dev, _, topics = partial.shape

    def finish(row, carry):
        value = finished(weights, extended, columns, scales, partial, row)
        following[row] = (spread_over(scales[row], topics) * value).astype(jnp.bfloat16)
        return carry

    def start(row, carry):
        next_partial[row] = near(weights, following, columns, scales, counts, row)
        return carry

    lax.fori_loop(0, blocks_dev, finish, 0, unroll=unroll)
    lax.fori_loop(0, blocks_dev, start, 0, unroll=unroll)


def last_body(
    columns, odd_x, odd_y, weights, extended_in, scales, partial, r0, r1, r2, r3, out, extended, block, sem, out_sem, *, chunk
):
    blocks_dev = partial.shape[0]
    chunks = blocks_dev // chunk
    arrivals((r0, r1, r2, r3), extended, odd_x, odd_y, sem)

    def leave(c):
        part = pl.ds(c * chunk, chunk)
        return pltpu.make_async_copy(block.at[part], out.at[part], out_sem.at[c])

    def step(c, carry):
        for i in range(chunk):
            row = c * chunk + i
            block[row] = finished(weights, extended, columns, scales, partial, row)
        leave(c).start()
        return carry

    lax.fori_loop(0, chunks, step, 0)
    for c in range(chunks):
        leave(c).wait()


def swap_pairs(axis, first):
    outer, inner = lax.axis_size("gx"), lax.axis_size("gy")
    count, other = (outer, inner) if axis == "gx" else (inner, outer)
    lines = []
    for low in range(first, count - 1, 2):
        lines += [((low, line), (low + 1, line)) for line in range(other)]
    alone = [place for place in range(count) if all(place not in (p[0], q[0]) for p, q in lines)]
    half = 1 if axis == "gx" else other // 2
    for place in alone:
        for line in range(other):
            if line // half % 2 == 0 and line + half < other:
                lines.append(((place, line), (place, line + half)))
    number = (lambda place, line: place * inner + line) if axis == "gx" else (lambda place, line: line * inner + place)
    pairs = []
    for p, q in lines:
        low, high = number(*p), number(*q)
        pairs += [(low, high), (high, low)]
    return sorted(pairs)


def swapped(value, axis, first):
    return lax.ppermute(value, ("gx", "gy"), swap_pairs(axis, first))


def local(labels, weights, column_index, send_index, seed_doc, seed_topic):
    blocks_dev, slots, block_size, _ = weights.shape
    documents = blocks_dev * block_size
    topics = labels.shape[1]
    sends = send_index.shape[2]
    seeds = seed_doc.shape[0]
    labels = labels.reshape(blocks_dev, block_size, topics)
    seed_doc = seed_doc.reshape(1, seeds)
    seed_topic = seed_topic.reshape(1, seeds)
    columns = column_index.T
    odd_x = (lax.axis_index("gx") % 2).reshape(1)
    odd_y = (lax.axis_index("gy") % 2).reshape(1)

    sent = VMEM((sends, block_size, topics), jnp.bfloat16)
    extended_shape = VMEM((blocks_dev + 4 * sends, block_size, topics), jnp.bfloat16)
    scale_shape = VMEM((blocks_dev, block_size, block_size), jnp.float32)
    count_shape = VMEM((blocks_dev, block_size, topics), jnp.bfloat16)
    partial_shape = VMEM((blocks_dev, block_size, topics), jnp.float32)

    xa, xb = call(
        first_send_body,
        (sent, sent),
        (IN_VMEM, IN_VMEM),
        (IN_SMEM, IN_SMEM, ANYWHERE, ANYWHERE),
        (
            pltpu.VMEM((2 * sends, slots, block_size, block_size), jnp.bfloat16),
            pltpu.VMEM((2 * sends, block_size, topics), jnp.float32),
            pltpu.SemaphoreType.DMA((2 * sends, 2)),
        ),
    )(send_index, odd_x, unmoved(weights), unmoved(labels))
    xa, xb = swapped(xa, "gx", 0), swapped(xb, "gx", 1)

    held, extended, scales, counts, ya, yb = call(
        functools.partial(degree_body, chunk=4),
        (VMEM(weights.shape, jnp.bfloat16), extended_shape, scale_shape, count_shape, sent, sent),
        (IN_VMEM,) * 6,
        (IN_SMEM,) * 2 + (IN_VMEM,) * 2 + (ANYWHERE,) * 2,
        (
            pltpu.VMEM((blocks_dev, block_size, topics), jnp.float32),
            pltpu.VMEM((seeds, topics), jnp.bfloat16),
            pltpu.SemaphoreType.DMA((blocks_dev // 4, 2)),
        ),
    )(send_index, odd_y, seed_doc, seed_topic, unmoved(weights), unmoved(labels))
    ya, yb = swapped(ya, "gy", 0), swapped(yb, "gy", 1)
    held, scales, counts = pinned(held), pinned(scales), pinned(counts)

    partial = call(
        functools.partial(near_body, unroll=16),
        partial_shape,
        IN_VMEM,
        (IN_SMEM,) + (IN_VMEM,) * 4,
    )(columns, held, pinned(extended), scales, counts)
    xa, xb, ya, yb, extended = call(
        second_send_body,
        (sent, sent, sent, sent, extended_shape),
        (IN_VMEM,) * 5,
        (IN_SMEM,) * 4 + (IN_VMEM,) * 4 + (ANYWHERE,) * 4,
        (pltpu.SemaphoreType.DMA((4,)),),
        aliases={5: 4},
    )(columns, send_index, odd_x, odd_y, held, pinned(extended), scales, pinned(partial), xa, xb, ya, yb)
    xa, xb = swapped(xa, "gx", 0), swapped(xb, "gx", 1)
    ya, yb = swapped(ya, "gy", 0), swapped(yb, "gy", 1)

    following, partial = call(
        functools.partial(rest_body, unroll=16),
        (extended_shape, partial_shape),
        (IN_VMEM,) * 2,
        (IN_SMEM,) + (IN_VMEM,) * 5,
    )(columns, held, pinned(extended), scales, counts, pinned(partial))

    out, _ = call(
        functools.partial(last_body, chunk=4),
        (jax.ShapeDtypeStruct((blocks_dev, block_size, topics), jnp.float32), extended_shape),
        (ANYWHERE, IN_VMEM),
        (IN_SMEM,) * 3 + (IN_VMEM,) * 4 + (ANYWHERE,) * 4,
        (
            pltpu.VMEM((blocks_dev, block_size, topics), jnp.float32),
            pltpu.SemaphoreType.DMA((4,)),
            pltpu.SemaphoreType.DMA((blocks_dev // 4,)),
        ),
        aliases={4: 1},
    )(columns, odd_x, odd_y, held, pinned(following), scales, pinned(partial), xa, xb, ya, yb)
    return out.reshape(documents, topics)


def solution(mesh):
    in_specs = (
        P(("gx", "gy"), None),
        P(("gx", "gy"), None, None, None),
        P(("gx", "gy"), None),
        P(("gx", "gy"), None, None),
        P(("gx", "gy")),
        P(("gx", "gy")),
    )
    out_specs = P(("gx", "gy"), None)
    return jax.shard_map(local, mesh=mesh, in_specs=in_specs, out_specs=out_specs, check_vma=False)
```

```python
import functools

import jax
import jax.numpy as jnp
from jax import lax
from jax.experimental import pallas as pl
from jax.experimental.pallas import tpu as pltpu
from jax.sharding import PartitionSpec as P

ITERS = 2

ALPHA = 0.99
GAIN = 1.0 / (1.0 - 0.99)
SEED_WEIGHT = (1.0 - ALPHA) * GAIN

LOCAL = 8
VMEM = pltpu.VMEM
IN_VMEM = pl.BlockSpec(memory_space=pltpu.VMEM)
IN_SMEM = pl.BlockSpec(memory_space=pltpu.SMEM)
ANYWHERE = pl.BlockSpec(memory_space=pl.ANY)


def call(body, out_shape, out_specs, in_specs, scratch=(), aliases=None, limit=8):
    return pl.pallas_call(
        body,
        out_shape=out_shape,
        in_specs=in_specs,
        out_specs=out_specs,
        scratch_shapes=scratch,
        input_output_aliases=aliases or {},
        compiler_params=pltpu.CompilerParams(vmem_limit_bytes=limit * 2**20),
        cost_estimate=pl.CostEstimate(flops=1, bytes_accessed=1, transcendentals=0),
    )


def pinned(value):
    return pltpu.with_memory_space_constraint(value, pltpu.VMEM)


def unmoved(value):
    return pltpu.with_memory_space_constraint(value, pltpu.HBM)


def tabled(value):
    return pltpu.with_memory_space_constraint(value, pltpu.SMEM)


def row_scale(weights, row):
    slots = weights.shape[1]
    total = weights[row, 0].astype(jnp.float32)
    for slot in range(1, slots):
        total = total + weights[row, slot].astype(jnp.float32)
    return lax.rsqrt(jnp.sum(total, axis=1, keepdims=True))


def spread_over(scale, width):
    return jnp.concatenate([scale] * (width // scale.shape[1]), axis=1)


def toward_x():
    turn = lax.axis_index("gx") % 2
    return (3 - turn, 2 + turn)


def toward_y():
    turn = lax.axis_index("gy") % 2
    return (1 - turn, turn)


def sent_row(send_index, order, sends, i):
    return send_index[0, order[i // sends], i % sends]


def weighted(weights, extended, columns, row, first, last):
    left = jnp.concatenate([weights[row, slot] for slot in range(first, last)], axis=1)
    right = jnp.concatenate([extended[columns[slot, row]] for slot in range(first, last)], axis=0)
    return jnp.dot(left, right, preferred_element_type=jnp.float32)


def row_copies(weights, labels, held, block, sem, row, slot):
    return (
        pltpu.make_async_copy(weights.at[row], held.at[row], sem.at[slot, 0]),
        pltpu.make_async_copy(labels.at[row], block.at[slot], sem.at[slot, 1]),
    )


def scale_row(held, block, extended, scales, row, slot):
    scale = row_scale(held, row)
    scales[row] = jnp.broadcast_to(scale, scales.shape[1:])
    extended[row] = (scale * block[slot]).astype(jnp.bfloat16)


def copy_out(source, send_index, order, outs):
    sends = send_index.shape[2]
    i = 0
    for out in outs:
        for j in range(out.shape[0]):
            out[j] = source[sent_row(send_index, order, sends, i)]
            i += 1


def first_send_body(
    column_index, send_index, weights, labels, x_a, x_b, held, extended, scales, columns, lists,
    block, seen, fresh, sem, table_sem,
):
    blocks_dev = held.shape[0]
    get_lists = pltpu.make_async_copy(send_index, lists, table_sem.at[0])
    get_columns = pltpu.make_async_copy(column_index, columns, table_sem.at[1])
    get_lists.start()
    get_columns.start()

    def unseen(row, carry):
        seen[row] = 0
        return carry

    lax.fori_loop(0, blocks_dev, unseen, 0, unroll=8)
    get_lists.wait()
    sends = lists.shape[2]
    order = toward_x()
    rows = [sent_row(lists, order, sends, i) for i in range(len(order) * sends)]
    for i, row in enumerate(rows):
        fresh[i] = 1 - seen[row]
        seen[row] = 1

        @pl.when(fresh[i] == 1)
        def _():
            for copy in row_copies(weights, labels, held, block, sem, row, i):
                copy.start()

    for i, row in enumerate(rows):

        @pl.when(fresh[i] == 1)
        def _():
            for copy in row_copies(weights, labels, held, block, sem, row, i):
                copy.wait()
            scale_row(held, block, extended, scales, row, i)

    copy_out(extended, lists, order, (x_a, x_b))
    get_columns.wait()


def degree_body(
    lists, seed_doc, seed_topic, weights, labels, held_in, extended_in, scales_in,
    held, extended, scales, counts, y_a, y_b, block, topic_hot, seen, left, sem, *, chunk,
):
    blocks_dev, block_size, topics = block.shape
    seeds = seed_doc.shape[1]

    def unseen(row, carry):
        seen[row] = 0
        return carry

    lax.fori_loop(0, blocks_dev, unseen, 0, unroll=8)
    for direction in toward_x():
        for i in range(lists.shape[2]):
            seen[lists[0, direction, i]] = 1

    def fetch(row, number):
        @pl.when(seen[row] == 0)
        def _():
            left[number] = row
            for copy in row_copies(weights, labels, held, block, sem, row, number):
                copy.start()

        return number + 1 - seen[row]

    number = lax.fori_loop(0, blocks_dev, fetch, jnp.int32(0))
    topic = lax.broadcasted_iota(jnp.int32, (topics, seeds), 0)
    hot = jnp.where(topic == seed_topic[...], 1.0, 0.0).astype(jnp.float32)
    topic_hot[...] = hot.T.astype(jnp.bfloat16)

    def count(row, carry):
        document = lax.broadcasted_iota(jnp.int32, (block_size, seeds), 0) + row * block_size
        doc_hot = jnp.where(document == seed_doc[...], 1.0, 0.0).astype(jnp.bfloat16)
        hits = jnp.dot(doc_hot, topic_hot[...], preferred_element_type=jnp.float32)
        counts[row] = hits.astype(jnp.bfloat16)
        return carry

    lax.fori_loop(0, blocks_dev, count, 0, unroll=8)

    def step(c, carry):
        slots = [jnp.minimum(c * chunk + i, number - 1) for i in range(chunk)]
        for i, slot in enumerate(slots):

            @pl.when(c * chunk + i < number)
            def _():
                for copy in row_copies(weights, labels, held, block, sem, left[slot], slot):
                    copy.wait()

        for slot in slots:
            scale_row(held, block, extended, scales, left[slot], slot)
        return carry

    lax.fori_loop(0, lax.div(number + chunk - 1, jnp.int32(chunk)), step, 0)
    copy_out(extended, lists, toward_y(), (y_a, y_b))


def near(weights, extended, columns, scales, counts, row):
    topics = extended.shape[2]
    product = weighted(weights, extended, columns, row, 0, LOCAL)
    return spread_over(ALPHA * scales[row], topics) * product + SEED_WEIGHT * counts[row].astype(jnp.float32)


def near_body(columns, weights, extended, scales, counts, partial, *, unroll):
    def step(row, carry):
        partial[row] = near(weights, extended, columns, scales, counts, row)
        return carry

    lax.fori_loop(0, partial.shape[0], step, 0, unroll=unroll)


def arrivals(pieces, extended):
    sends = pieces[0].shape[0]
    low = extended.shape[0] - 4 * sends
    order = toward_x() + toward_y()
    i = 0
    for piece in pieces:
        extended[pl.ds(low + order[i // sends] * sends + i % sends, piece.shape[0])] = piece[...]
        i += piece.shape[0]


def finished(weights, extended, columns, scales, partial, row):
    topics = partial.shape[2]
    slots = weights.shape[1]
    product = weighted(weights, extended, columns, row, LOCAL, slots)
    return partial[row] + spread_over(ALPHA * scales[row], topics) * product


def second_send_body(
    columns, lists, weights, extended_in, scales, partial, r0, r1, r2, r3, x_a, x_b, x_c, y_a, y_b, extended
):
    sends = lists.shape[2]
    topics = x_a.shape[2]
    arrivals((r0, r1, r2, r3), extended)
    order = toward_x() + toward_y()
    i = 0
    for out in (x_a, x_b, x_c, y_a, y_b):
        for j in range(out.shape[0]):
            row = sent_row(lists, order, sends, i)
            value = finished(weights, extended, columns, scales, partial, row)
            out[j] = (spread_over(scales[row], topics) * value).astype(jnp.bfloat16)
            i += 1


def rest_body(columns, weights, extended, scales, partial, following, *, unroll):
    blocks_dev, _, topics = partial.shape

    def finish(row, carry):
        value = finished(weights, extended, columns, scales, partial, row)
        following[row] = (spread_over(scales[row], topics) * value).astype(jnp.bfloat16)
        return carry

    lax.fori_loop(0, blocks_dev, finish, 0, unroll=unroll)


def last_body(
    columns, weights, extended_in, scales, partial, r0, r1, r2, r3, r4, out, extended, block, sem, *, unroll
):
    blocks_dev = partial.shape[0]
    arrivals((r0, r1, r2, r3, r4), extended)

    def leave(row):
        return pltpu.make_async_copy(block.at[row], out.at[row], sem.at[row])

    def step(row, carry):
        block[row] = finished(weights, extended, columns, scales, partial, row)
        leave(row).start()
        return carry

    lax.fori_loop(0, blocks_dev, step, 0, unroll=unroll)

    def settle(row, carry):
        leave(row).wait()
        return carry

    lax.fori_loop(0, blocks_dev, settle, 0)


def swap_pairs(axis, first):
    outer, inner = lax.axis_size("gx"), lax.axis_size("gy")
    count, other = (outer, inner) if axis == "gx" else (inner, outer)
    lines = []
    for low in range(first, count - 1, 2):
        lines += [((low, line), (low + 1, line)) for line in range(other)]
    alone = [place for place in range(count) if all(place not in (p[0], q[0]) for p, q in lines)]
    half = 1 if axis == "gx" else other // 2
    for place in alone:
        for line in range(other):
            if line // half % 2 == 0 and line + half < other:
                lines.append(((place, line), (place, line + half)))
    number = (lambda place, line: place * inner + line) if axis == "gx" else (lambda place, line: line * inner + place)
    pairs = []
    for p, q in lines:
        low, high = number(*p), number(*q)
        pairs += [(low, high), (high, low)]
    return sorted(pairs)


def swapped(value, axis, first):
    return lax.ppermute(value, ("gx", "gy"), swap_pairs(axis, first))


def relayed(value):
    if lax.axis_size("gx") != 4:
        return swapped(value, "gx", 1)
    value = lax.ppermute(value, "gx", [(0, 2), (1, 3), (2, 0), (3, 1)])
    return lax.ppermute(value, "gx", [(0, 1), (1, 3), (3, 2), (2, 0)])


def local(labels, weights, column_index, send_index, seed_doc, seed_topic):
    blocks_dev, slots, block_size, _ = weights.shape
    documents = blocks_dev * block_size
    topics = labels.shape[1]
    sends = send_index.shape[2]
    seeds = seed_doc.shape[0]
    labels = unmoved(labels.reshape(blocks_dev, block_size, topics))
    weights = unmoved(weights)
    send_index = unmoved(send_index)
    seed_doc = seed_doc.reshape(1, seeds)
    seed_topic = seed_topic.reshape(1, seeds)
    half = sends // 2
    whole = VMEM((sends, block_size, topics), jnp.bfloat16)
    first_half = VMEM((half, block_size, topics), jnp.bfloat16)
    second_half = VMEM((sends - half, block_size, topics), jnp.bfloat16)
    held_shape = VMEM(weights.shape, jnp.bfloat16)
    extended_shape = VMEM((blocks_dev + 4 * sends, block_size, topics), jnp.bfloat16)
    scale_shape = VMEM((blocks_dev, block_size, block_size), jnp.float32)
    count_shape = VMEM((blocks_dev, block_size, topics), jnp.bfloat16)
    partial_shape = VMEM((blocks_dev, block_size, topics), jnp.float32)

    x_a, x_b, held, extended, scales, columns, lists = call(
        first_send_body,
        (whole, whole, held_shape, extended_shape, scale_shape)
        + (pltpu.SMEM((slots, blocks_dev), jnp.int32), pltpu.SMEM(send_index.shape, jnp.int32)),
        (IN_VMEM,) * 5 + (IN_SMEM,) * 2,
        (ANYWHERE,) * 4,
        (
            pltpu.VMEM((2 * sends, block_size, topics), jnp.float32),
            pltpu.SMEM((blocks_dev,), jnp.int32),
            pltpu.SMEM((2 * sends,), jnp.int32),
            pltpu.SemaphoreType.DMA((2 * sends, 2)),
            pltpu.SemaphoreType.DMA((2,)),
        ),
    )(unmoved(column_index.T), send_index, weights, labels)
    x_a, x_b = swapped(x_a, "gx", 0), swapped(x_b, "gx", 1)
    columns, lists = tabled(columns), tabled(lists)

    held, extended, scales, counts, y_a, y_b = call(
        functools.partial(degree_body, chunk=4),
        (held_shape, extended_shape, scale_shape, count_shape, whole, whole),
        (IN_VMEM,) * 6,
        (IN_SMEM,) + (IN_VMEM,) * 2 + (ANYWHERE,) * 2 + (IN_VMEM,) * 3,
        (
            pltpu.VMEM((blocks_dev, block_size, topics), jnp.float32),
            pltpu.VMEM((seeds, topics), jnp.bfloat16),
            pltpu.SMEM((blocks_dev,), jnp.int32),
            pltpu.SMEM((blocks_dev,), jnp.int32),
            pltpu.SemaphoreType.DMA((blocks_dev, 2)),
        ),
        aliases={5: 0, 6: 1, 7: 2},
    )(lists, seed_doc, seed_topic, weights, labels, pinned(held), pinned(extended), pinned(scales))
    y_b, y_a = swapped(y_b, "gy", 1), swapped(y_a, "gy", 0)
    held, scales, counts = pinned(held), pinned(scales), pinned(counts)

    def started(extended):
        return call(
            functools.partial(near_body, unroll=16),
            partial_shape,
            IN_VMEM,
            (IN_SMEM,) + (IN_VMEM,) * 4,
        )(columns, held, pinned(extended), scales, counts)

    partial = started(extended)
    x_a, x_b, x_c, y_a, y_b, extended = call(
        second_send_body,
        (whole, first_half, second_half, whole, whole, extended_shape),
        (IN_VMEM,) * 6,
        (IN_SMEM,) * 2 + (IN_VMEM,) * 8,
        aliases={3: 5},
    )(columns, lists, held, pinned(extended), scales, pinned(partial), *map(pinned, (x_a, x_b, y_a, y_b)))
    x_c, x_a, x_b = relayed(x_c), swapped(x_a, "gx", 0), swapped(x_b, "gx", 1)
    y_b, y_a = swapped(y_b, "gy", 1), swapped(y_a, "gy", 0)

    following = call(
        functools.partial(rest_body, unroll=16),
        extended_shape,
        IN_VMEM,
        (IN_SMEM,) + (IN_VMEM,) * 4,
    )(columns, held, pinned(extended), scales, pinned(partial))
    partial = started(following)

    out, _ = call(
        functools.partial(last_body, unroll=16),
        (jax.ShapeDtypeStruct((blocks_dev, block_size, topics), jnp.float32), extended_shape),
        (ANYWHERE, IN_VMEM),
        (IN_SMEM,) + (IN_VMEM,) * 9,
        (
            pltpu.VMEM((blocks_dev, block_size, topics), jnp.float32),
            pltpu.SemaphoreType.DMA((blocks_dev,)),
        ),
        aliases={2: 1},
    )(columns, held, pinned(following), scales, pinned(partial), *map(pinned, (x_a, x_b, x_c, y_a, y_b)))
    return out.reshape(documents, topics)


def solution(mesh):
    in_specs = (
        P(("gx", "gy"), None),
        P(("gx", "gy"), None, None, None),
        P(("gx", "gy"), None),
        P(("gx", "gy"), None, None),
        P(("gx", "gy")),
        P(("gx", "gy")),
    )
    out_specs = P(("gx", "gy"), None)
    return jax.shard_map(local, mesh=mesh, in_specs=in_specs, out_specs=out_specs, check_vma=False)
```

```python
import functools

import jax
import jax.numpy as jnp
from jax import lax
from jax.experimental import pallas as pl
from jax.experimental.pallas import tpu as pltpu
from jax.sharding import PartitionSpec as P

ITERS = 2

ALPHA = 0.99
GAIN = 1.0 / (1.0 - 0.99)
SEED_WEIGHT = (1.0 - ALPHA) * GAIN

EARLY = 4
LOCAL = 8
VMEM = pltpu.VMEM
IN_VMEM = pl.BlockSpec(memory_space=pltpu.VMEM)
IN_SMEM = pl.BlockSpec(memory_space=pltpu.SMEM)
ANYWHERE = pl.BlockSpec(memory_space=pl.ANY)


def call(body, out_shape, out_specs, in_specs, scratch=(), aliases=None, limit=8):
    return pl.pallas_call(
        body,
        out_shape=out_shape,
        in_specs=in_specs,
        out_specs=out_specs,
        scratch_shapes=scratch,
        input_output_aliases=aliases or {},
        compiler_params=pltpu.CompilerParams(vmem_limit_bytes=limit * 2**20),
        cost_estimate=pl.CostEstimate(flops=1, bytes_accessed=1, transcendentals=0),
    )


def pinned(value):
    return pltpu.with_memory_space_constraint(value, pltpu.VMEM)


def unmoved(value):
    return pltpu.with_memory_space_constraint(value, pltpu.HBM)


def tabled(value):
    return pltpu.with_memory_space_constraint(value, pltpu.SMEM)


def row_scale(weights, row):
    slots = weights.shape[1]
    total = weights[row, 0].astype(jnp.float32)
    for slot in range(1, slots):
        total = total + weights[row, slot].astype(jnp.float32)
    return lax.rsqrt(jnp.sum(total, axis=1, keepdims=True))


def spread_over(scale, width):
    return jnp.concatenate([scale] * (width // scale.shape[1]), axis=1)


def toward_x():
    turn = lax.axis_index("gx") % 2
    return (3 - turn, 2 + turn)


def toward_y():
    turn = lax.axis_index("gy") % 2
    return (1 - turn, turn)


def sent_row(send_index, order, sends, i):
    return send_index[0, order[i // sends], i % sends]


def weighted(weights, extended, columns, row, first, last):
    left = jnp.concatenate([weights[row, slot] for slot in range(first, last)], axis=1)
    right = jnp.concatenate([extended[columns[slot, row]] for slot in range(first, last)], axis=0)
    return jnp.dot(left, right, preferred_element_type=jnp.float32)


def row_copies(weights, labels, held, block, sem, row, slot):
    return (
        pltpu.make_async_copy(weights.at[row], held.at[row], sem.at[slot, 0]),
        pltpu.make_async_copy(labels.at[row], block.at[slot], sem.at[slot, 1]),
    )


def scale_row(held, block, extended, scales, row, slot):
    scale = row_scale(held, row)
    scales[row] = jnp.broadcast_to(scale, scales.shape[1:])
    extended[row] = (scale * block[slot]).astype(jnp.bfloat16)


def copy_out(source, send_index, order, outs):
    sends = send_index.shape[2]
    i = 0
    for out in outs:
        for j in range(out.shape[0]):
            out[j] = source[sent_row(send_index, order, sends, i)]
            i += 1


def first_send_body(
    column_index, send_index, weights, labels, x_a, x_b, held, extended, scales, columns, lists,
    block, seen, fresh, sem, table_sem,
):
    blocks_dev = held.shape[0]
    get_lists = pltpu.make_async_copy(send_index, lists, table_sem.at[0])
    get_columns = pltpu.make_async_copy(column_index, columns, table_sem.at[1])
    get_lists.start()
    get_columns.start()

    def unseen(row, carry):
        seen[row] = 0
        return carry

    sends = x_a.shape[0]
    early = block.shape[0] - 2 * sends
    for row in range(early):
        for copy in row_copies(weights, labels, held, block, sem, row, 2 * sends + row):
            copy.start()
    lax.fori_loop(0, blocks_dev, unseen, 0, unroll=8)
    for row in range(early):
        seen[row] = 1
    get_lists.wait()
    order = toward_x()
    rows = [sent_row(lists, order, sends, i) for i in range(len(order) * sends)]
    for i, row in enumerate(rows):
        fresh[i] = 1 - seen[row]
        seen[row] = 1

        @pl.when(fresh[i] == 1)
        def _():
            for copy in row_copies(weights, labels, held, block, sem, row, i):
                copy.start()

    for row in range(early):
        for copy in row_copies(weights, labels, held, block, sem, row, 2 * sends + row):
            copy.wait()
    for row in range(early):
        scale_row(held, block, extended, scales, row, 2 * sends + row)
    for i, row in enumerate(rows):

        @pl.when(fresh[i] == 1)
        def _():
            for copy in row_copies(weights, labels, held, block, sem, row, i):
                copy.wait()
            scale_row(held, block, extended, scales, row, i)

    copy_out(extended, lists, order, (x_a, x_b))
    get_columns.wait()


def degree_body(
    lists, seed_doc, seed_topic, weights, labels, held_in, extended_in, scales_in,
    held, extended, scales, counts, y_a, y_b, block, topic_hot, seen, left, sem, *, chunk,
):
    blocks_dev, block_size, topics = block.shape
    seeds = seed_doc.shape[1]

    def unseen(row, carry):
        seen[row] = 0
        return carry

    lax.fori_loop(0, blocks_dev, unseen, 0, unroll=8)
    for direction in toward_x():
        for i in range(lists.shape[2]):
            seen[lists[0, direction, i]] = 1
    for row in range(EARLY):
        seen[row] = 1

    def fetch(row, number):
        @pl.when(seen[row] == 0)
        def _():
            left[number] = row
            for copy in row_copies(weights, labels, held, block, sem, row, number):
                copy.start()

        return number + 1 - seen[row]

    number = lax.fori_loop(0, blocks_dev, fetch, jnp.int32(0))
    topic = lax.broadcasted_iota(jnp.int32, (topics, seeds), 0)
    hot = jnp.where(topic == seed_topic[...], 1.0, 0.0).astype(jnp.float32)
    topic_hot[...] = hot.T.astype(jnp.bfloat16)

    def count(row, carry):
        document = lax.broadcasted_iota(jnp.int32, (block_size, seeds), 0) + row * block_size
        doc_hot = jnp.where(document == seed_doc[...], 1.0, 0.0).astype(jnp.bfloat16)
        hits = jnp.dot(doc_hot, topic_hot[...], preferred_element_type=jnp.float32)
        counts[row] = hits.astype(jnp.bfloat16)
        return carry

    lax.fori_loop(0, blocks_dev, count, 0, unroll=8)

    def step(c, carry):
        slots = [jnp.minimum(c * chunk + i, number - 1) for i in range(chunk)]
        for i, slot in enumerate(slots):

            @pl.when(c * chunk + i < number)
            def _():
                for copy in row_copies(weights, labels, held, block, sem, left[slot], slot):
                    copy.wait()

        for slot in slots:
            scale_row(held, block, extended, scales, left[slot], slot)
        return carry

    lax.fori_loop(0, lax.div(number + chunk - 1, jnp.int32(chunk)), step, 0)
    copy_out(extended, lists, toward_y(), (y_a, y_b))


def pick_body(lists, source, out, *, number):
    direction = toward_y()[number]
    for i in range(out.shape[0]):
        out[i] = source[lists[0, direction, i]]


def near(weights, extended, columns, scales, counts, row):
    topics = extended.shape[2]
    product = weighted(weights, extended, columns, row, 0, LOCAL)
    return spread_over(ALPHA * scales[row], topics) * product + SEED_WEIGHT * counts[row].astype(jnp.float32)


def near_body(columns, weights, extended, scales, counts, *rest, unroll):
    partial = rest[-1]

    def step(row, carry):
        partial[row] = near(weights, extended, columns, scales, counts, row)
        return carry

    lax.fori_loop(0, partial.shape[0], step, 0, unroll=unroll)


def arrivals(pieces, extended):
    sends = pieces[0].shape[0]
    low = extended.shape[0] - 4 * sends
    order = toward_x() + toward_y()
    i = 0
    for piece in pieces:
        extended[pl.ds(low + order[i // sends] * sends + i % sends, piece.shape[0])] = piece[...]
        i += piece.shape[0]


def finished(weights, extended, columns, scales, partial, row):
    topics = partial.shape[2]
    slots = weights.shape[1]
    product = weighted(weights, extended, columns, row, LOCAL, slots)
    return partial[row] + spread_over(ALPHA * scales[row], topics) * product


def second_send_body(
    columns, lists, weights, extended_in, scales, partial, r0, r1, r2, r3, x_a, x_b, extended
):
    sends = lists.shape[2]
    topics = x_a.shape[2]
    arrivals((r0, r1, r2, r3), extended)
    order = toward_x()
    i = 0
    for out in (x_a, x_b):
        for j in range(out.shape[0]):
            row = sent_row(lists, order, sends, i)
            value = finished(weights, extended, columns, scales, partial, row)
            out[j] = (spread_over(scales[row], topics) * value).astype(jnp.bfloat16)
            i += 1


def rest_body(columns, lists, weights, extended, scales, partial, following, y_a, y_b, handed, *, unroll):
    blocks_dev, _, topics = partial.shape

    def finish(row, carry):
        value = finished(weights, extended, columns, scales, partial, row)
        following[row] = (spread_over(scales[row], topics) * value).astype(jnp.bfloat16)
        return carry

    lax.fori_loop(0, blocks_dev, finish, 0, unroll=unroll)
    copy_out(following, lists, toward_y(), (y_a, y_b))


def last_body(
    columns, weights, extended_in, scales, partial, r0, r1, r2, r3, out, extended, block, sem, *, unroll
):
    blocks_dev = partial.shape[0]
    arrivals((r0, r1, r2, r3), extended)

    def leave(row):
        return pltpu.make_async_copy(block.at[row], out.at[row], sem.at[row])

    def step(row, carry):
        block[row] = finished(weights, extended, columns, scales, partial, row)
        leave(row).start()
        return carry

    lax.fori_loop(0, blocks_dev, step, 0, unroll=unroll)

    def settle(row, carry):
        leave(row).wait()
        return carry

    lax.fori_loop(0, blocks_dev, settle, 0)


ROUND = ((0, 1), (1, 3), (3, 2), (2, 0))


def neighbours(count, first):
    pairs = [p for low in range(first, count - 1, 2) for p in ((low, low + 1), (low + 1, low))]
    return pairs, [place for place in range(count) if all(place != source for source, _ in pairs)]


def permuted(value, pairs):
    inner = lax.axis_size("gy")
    return lax.ppermute(value, ("gx", "gy"), sorted((a * inner + b, c * inner + d) for (a, b), (c, d) in pairs))


def along_x(line, pairs):
    return [((source, line), (target, line)) for source, target in pairs]


def along_y(line, pairs):
    return [((line, source), (line, target)) for source, target in pairs]


def x_swap(value, first):
    outer, inner = lax.axis_size("gx"), lax.axis_size("gy")
    pairs, alone = neighbours(outer, first)
    moves = [move for line in range(inner) for move in along_x(line, pairs)]
    moves += [move for place in alone for move in along_y(place, neighbours(inner, 0)[0])]
    return permuted(value, moves)


def y_swap(value, first, whole=True):
    outer, inner = lax.axis_size("gx"), lax.axis_size("gy")
    pairs, alone = neighbours(inner, first)
    moves = [move for line in range(outer) for move in along_y(line, pairs)]
    if whole:
        moves += [move for place in alone for move in along_x(place, ROUND if outer == 4 else neighbours(outer, 0)[0])]
    return permuted(value, moves)


def local(labels, weights, column_index, send_index, seed_doc, seed_topic):
    blocks_dev, slots, block_size, _ = weights.shape
    documents = blocks_dev * block_size
    topics = labels.shape[1]
    sends = send_index.shape[2]
    seeds = seed_doc.shape[0]
    labels = unmoved(labels.reshape(blocks_dev, block_size, topics))
    weights = unmoved(weights)
    send_index = unmoved(send_index)
    seed_doc = seed_doc.reshape(1, seeds)
    seed_topic = seed_topic.reshape(1, seeds)
    whole = VMEM((sends, block_size, topics), jnp.bfloat16)
    held_shape = VMEM(weights.shape, jnp.bfloat16)
    extended_shape = VMEM((blocks_dev + 4 * sends, block_size, topics), jnp.bfloat16)
    scale_shape = VMEM((blocks_dev, block_size, block_size), jnp.float32)
    count_shape = VMEM((blocks_dev, block_size, topics), jnp.bfloat16)
    partial_shape = VMEM((blocks_dev, block_size, topics), jnp.float32)

    x_a, x_b, held, extended, scales, columns, lists = call(
        first_send_body,
        (whole, whole, held_shape, extended_shape, scale_shape)
        + (pltpu.SMEM((slots, blocks_dev), jnp.int32), pltpu.SMEM(send_index.shape, jnp.int32)),
        (IN_VMEM,) * 5 + (IN_SMEM,) * 2,
        (ANYWHERE,) * 4,
        (
            pltpu.VMEM((2 * sends + EARLY, block_size, topics), jnp.float32),
            pltpu.SMEM((blocks_dev,), jnp.int32),
            pltpu.SMEM((2 * sends,), jnp.int32),
            pltpu.SemaphoreType.DMA((2 * sends + EARLY, 2)),
            pltpu.SemaphoreType.DMA((2,)),
        ),
    )(unmoved(column_index.T), send_index, weights, labels)
    x_a, x_b = x_swap(x_a, 0), x_swap(x_b, 1)
    columns, lists = tabled(columns), tabled(lists)

    held, extended, scales, counts, y_a, y_b = call(
        functools.partial(degree_body, chunk=4),
        (held_shape, extended_shape, scale_shape, count_shape, whole, whole),
        (IN_VMEM,) * 6,
        (IN_SMEM,) + (IN_VMEM,) * 2 + (ANYWHERE,) * 2 + (IN_VMEM,) * 3,
        (
            pltpu.VMEM((blocks_dev, block_size, topics), jnp.float32),
            pltpu.VMEM((seeds, topics), jnp.bfloat16),
            pltpu.SMEM((blocks_dev,), jnp.int32),
            pltpu.SMEM((blocks_dev,), jnp.int32),
            pltpu.SemaphoreType.DMA((blocks_dev, 2)),
        ),
        aliases={5: 0, 6: 1, 7: 2},
    )(lists, seed_doc, seed_topic, weights, labels, pinned(held), pinned(extended), pinned(scales))
    y_a, y_b = y_swap(y_a, 0), y_swap(y_b, 1)
    held, scales, counts = pinned(held), pinned(scales), pinned(counts)

    def started(extended, *reused):
        return call(
            functools.partial(near_body, unroll=16),
            partial_shape,
            IN_VMEM,
            (IN_SMEM,) + (IN_VMEM,) * (4 + len(reused)),
            aliases={4 + len(reused): 0} if reused else {},
        )(columns, held, pinned(extended), scales, counts, *reused)

    partial = started(extended)
    x_a, x_b, extended = call(
        second_send_body,
        (whole, whole, extended_shape),
        (IN_VMEM,) * 3,
        (IN_SMEM,) * 2 + (IN_VMEM,) * 8,
        aliases={3: 2},
    )(columns, lists, held, pinned(extended), scales, pinned(partial), *map(pinned, (x_a, x_b, y_a, y_b)))
    x_a, x_b = x_swap(x_a, 0), x_swap(x_b, 1)

    following, y_a, y_b, partial = call(
        functools.partial(rest_body, unroll=16),
        (extended_shape, whole, whole, partial_shape),
        (IN_VMEM,) * 4,
        (IN_SMEM,) * 2 + (IN_VMEM,) * 4,
        aliases={5: 3},
    )(columns, lists, held, pinned(extended), scales, pinned(partial))
    y_a, y_b = y_swap(y_a, 0), y_swap(y_b, 1, whole=False)
    partial = started(following, pinned(extended), pinned(partial))

    out, _ = call(
        functools.partial(last_body, unroll=16),
        (jax.ShapeDtypeStruct((blocks_dev, block_size, topics), jnp.float32), extended_shape),
        (ANYWHERE, IN_VMEM),
        (IN_SMEM,) + (IN_VMEM,) * 8,
        (
            pltpu.VMEM((blocks_dev, block_size, topics), jnp.float32),
            pltpu.SemaphoreType.DMA((blocks_dev,)),
        ),
        aliases={2: 1},
    )(columns, held, pinned(following), scales, pinned(partial), *map(pinned, (x_a, x_b, y_a, y_b)))
    return out.reshape(documents, topics)


def solution(mesh):
    in_specs = (
        P(("gx", "gy"), None),
        P(("gx", "gy"), None, None, None),
        P(("gx", "gy"), None),
        P(("gx", "gy"), None, None),
        P(("gx", "gy")),
        P(("gx", "gy")),
    )
    out_specs = P(("gx", "gy"), None)
    return jax.shard_map(local, mesh=mesh, in_specs=in_specs, out_specs=out_specs, check_vma=False)
```

```python
import functools

import jax
import jax.numpy as jnp
from jax import lax
from jax.experimental import pallas as pl
from jax.experimental.pallas import tpu as pltpu
from jax.sharding import PartitionSpec as P

ITERS = 2

ALPHA = 0.99
GAIN = 1.0 / (1.0 - 0.99)
SEED_WEIGHT = (1.0 - ALPHA) * GAIN

EARLY = 4
LOCAL = 8
VMEM = pltpu.VMEM
IN_VMEM = pl.BlockSpec(memory_space=pltpu.VMEM)
IN_SMEM = pl.BlockSpec(memory_space=pltpu.SMEM)
ANYWHERE = pl.BlockSpec(memory_space=pl.ANY)


def call(body, out_shape, out_specs, in_specs, scratch=(), aliases=None, limit=8):
    return pl.pallas_call(
        body,
        out_shape=out_shape,
        in_specs=in_specs,
        out_specs=out_specs,
        scratch_shapes=scratch,
        input_output_aliases=aliases or {},
        compiler_params=pltpu.CompilerParams(vmem_limit_bytes=limit * 2**20),
        cost_estimate=pl.CostEstimate(flops=1, bytes_accessed=1, transcendentals=0),
    )


def pinned(value):
    return pltpu.with_memory_space_constraint(value, pltpu.VMEM)


def unmoved(value):
    return pltpu.with_memory_space_constraint(value, pltpu.HBM)


def tabled(value):
    return pltpu.with_memory_space_constraint(value, pltpu.SMEM)


def row_scale(weights, row):
    slots = weights.shape[1]
    total = weights[row, 0].astype(jnp.float32)
    for slot in range(1, slots):
        total = total + weights[row, slot].astype(jnp.float32)
    return lax.rsqrt(jnp.sum(total, axis=1, keepdims=True))


def spread_over(scale, width):
    return jnp.concatenate([scale] * (width // scale.shape[1]), axis=1)


def toward_x():
    turn = lax.axis_index("gx") % 2
    return (3 - turn, 2 + turn)


def toward_y():
    turn = lax.axis_index("gy") % 2
    return (1 - turn, turn)


def sent_row(send_index, order, sends, i):
    return send_index[0, order[i // sends], i % sends]


def weighted(weights, extended, columns, row, first, last):
    left = jnp.concatenate([weights[row, slot] for slot in range(first, last)], axis=1)
    right = jnp.concatenate([extended[columns[slot, row]] for slot in range(first, last)], axis=0)
    return jnp.dot(left, right, preferred_element_type=jnp.float32)


def row_copies(weights, labels, held, block, sem, row, slot):
    return (
        pltpu.make_async_copy(weights.at[row], held.at[row], sem.at[slot, 0]),
        pltpu.make_async_copy(labels.at[row], block.at[slot], sem.at[slot, 1]),
    )


def scale_row(held, block, extended, scales, row, slot):
    scale = row_scale(held, row)
    scales[row] = jnp.broadcast_to(scale, scales.shape[1:])
    extended[row] = (scale * block[slot]).astype(jnp.bfloat16)


def copy_out(source, send_index, order, outs):
    sends = send_index.shape[2]
    i = 0
    for out in outs:
        for j in range(out.shape[0]):
            out[j] = source[sent_row(send_index, order, sends, i)]
            i += 1


def first_send_body(
    column_index, send_index, weights, labels, x_a, x_b, held, extended, scales, columns, lists,
    block, seen, fresh, sem, table_sem,
):
    blocks_dev = held.shape[0]
    get_lists = pltpu.make_async_copy(send_index, lists, table_sem.at[0])
    get_columns = pltpu.make_async_copy(column_index, columns, table_sem.at[1])
    get_lists.start()
    get_columns.start()

    def unseen(row, carry):
        seen[row] = 0
        return carry

    sends = x_a.shape[0]
    early = block.shape[0] - 2 * sends
    for row in range(early):
        for copy in row_copies(weights, labels, held, block, sem, row, 2 * sends + row):
            copy.start()
    lax.fori_loop(0, blocks_dev, unseen, 0, unroll=8)
    for row in range(early):
        seen[row] = 1
    get_lists.wait()
    order = toward_x()
    rows = [sent_row(lists, order, sends, i) for i in range(len(order) * sends)]
    for i, row in enumerate(rows):
        fresh[i] = 1 - seen[row]
        seen[row] = 1

        @pl.when(fresh[i] == 1)
        def _():
            for copy in row_copies(weights, labels, held, block, sem, row, i):
                copy.start()

    for row in range(early):
        for copy in row_copies(weights, labels, held, block, sem, row, 2 * sends + row):
            copy.wait()
    for row in range(early):
        scale_row(held, block, extended, scales, row, 2 * sends + row)
    for i, row in enumerate(rows):

        @pl.when(fresh[i] == 1)
        def _():
            for copy in row_copies(weights, labels, held, block, sem, row, i):
                copy.wait()
            scale_row(held, block, extended, scales, row, i)

        out = x_a if i < sends else x_b
        out[i % sends] = extended[row]
    get_columns.wait()


def degree_body(
    lists, seed_doc, seed_topic, weights, labels, held_in, extended_in, scales_in,
    held, extended, scales, counts, y_a, y_b, block, topic_hot, seen, left, sem, *, chunk,
):
    blocks_dev, block_size, topics = block.shape
    seeds = seed_doc.shape[1]

    def unseen(row, carry):
        seen[row] = 0
        return carry

    lax.fori_loop(0, blocks_dev, unseen, 0, unroll=8)
    for direction in toward_x():
        for i in range(lists.shape[2]):
            seen[lists[0, direction, i]] = 1
    for row in range(EARLY):
        seen[row] = 1

    def fetch(row, number):
        @pl.when(seen[row] == 0)
        def _():
            left[number] = row
            for copy in row_copies(weights, labels, held, block, sem, row, number):
                copy.start()

        return number + 1 - seen[row]

    number = lax.fori_loop(0, blocks_dev, fetch, jnp.int32(0))
    topic = lax.broadcasted_iota(jnp.int32, (topics, seeds), 0)
    hot = jnp.where(topic == seed_topic[...], 1.0, 0.0).astype(jnp.float32)
    topic_hot[...] = hot.T.astype(jnp.bfloat16)

    def count(row, carry):
        document = lax.broadcasted_iota(jnp.int32, (block_size, seeds), 0) + row * block_size
        doc_hot = jnp.where(document == seed_doc[...], 1.0, 0.0).astype(jnp.bfloat16)
        hits = jnp.dot(doc_hot, topic_hot[...], preferred_element_type=jnp.float32)
        counts[row] = hits.astype(jnp.bfloat16)
        return carry

    lax.fori_loop(0, blocks_dev, count, 0, unroll=8)

    def step(c, carry):
        slots = [jnp.minimum(c * chunk + i, number - 1) for i in range(chunk)]
        for i, slot in enumerate(slots):

            @pl.when(c * chunk + i < number)
            def _():
                for copy in row_copies(weights, labels, held, block, sem, left[slot], slot):
                    copy.wait()

        for slot in slots:
            scale_row(held, block, extended, scales, left[slot], slot)
        return carry

    lax.fori_loop(0, lax.div(number + chunk - 1, jnp.int32(chunk)), step, 0)
    copy_out(extended, lists, toward_y(), (y_a, y_b))


def pick_body(lists, source, out, *, number):
    direction = toward_y()[number]
    for i in range(out.shape[0]):
        out[i] = source[lists[0, direction, i]]


def near(weights, extended, columns, scales, counts, row):
    topics = extended.shape[2]
    product = weighted(weights, extended, columns, row, 0, LOCAL)
    return spread_over(ALPHA * scales[row], topics) * product + SEED_WEIGHT * counts[row].astype(jnp.float32)


def near_body(columns, weights, extended, scales, counts, *rest, unroll):
    partial = rest[-1]

    def step(row, carry):
        partial[row] = near(weights, extended, columns, scales, counts, row)
        return carry

    lax.fori_loop(0, partial.shape[0], step, 0, unroll=unroll)


def arrivals(pieces, extended):
    sends = pieces[0].shape[0]
    low = extended.shape[0] - 4 * sends
    order = toward_x() + toward_y()
    i = 0
    for piece in pieces:
        extended[pl.ds(low + order[i // sends] * sends + i % sends, piece.shape[0])] = piece[...]
        i += piece.shape[0]


def finished(weights, extended, columns, scales, partial, row):
    topics = partial.shape[2]
    slots = weights.shape[1]
    product = weighted(weights, extended, columns, row, LOCAL, slots)
    return partial[row] + spread_over(ALPHA * scales[row], topics) * product


def second_send_body(
    columns, lists, weights, extended_in, scales, partial, r0, r1, r2, r3, x_a, x_b, y_a, y_b, extended
):
    sends = lists.shape[2]
    topics = x_a.shape[2]
    arrivals((r1, r0, r3, r2), extended)
    order = toward_x() + toward_y()
    for number, out in ((1, x_b), (0, x_a), (3, y_b), (2, y_a)):
        for i in range(sends):
            row = lists[0, order[number], i]
            value = finished(weights, extended, columns, scales, partial, row)
            out[i] = (spread_over(scales[row], topics) * value).astype(jnp.bfloat16)


def rest_body(columns, weights, extended, scales, partial, following, handed, *, unroll):
    blocks_dev, _, topics = partial.shape

    def finish(row, carry):
        value = finished(weights, extended, columns, scales, partial, row)
        following[row] = (spread_over(scales[row], topics) * value).astype(jnp.bfloat16)
        return carry

    lax.fori_loop(0, blocks_dev, finish, 0, unroll=unroll)


def hand_on_body(direct, first_hop, out):
    straight = lax.axis_index("gy") % 2 == 0

    @pl.when(straight)
    def _():
        out[...] = direct[...]

    @pl.when(jnp.logical_not(straight))
    def _():
        out[...] = first_hop[...]


def last_body(
    columns, weights, extended_in, scales, partial, r0, r1, r2, r3, out, extended, block, sem, *, unroll
):
    blocks_dev = partial.shape[0]
    arrivals((r0, r1, r2, r3), extended)

    def leave(row):
        return pltpu.make_async_copy(block.at[row], out.at[row], sem.at[row])

    def step(row, carry):
        block[row] = finished(weights, extended, columns, scales, partial, row)
        leave(row).start()
        return carry

    lax.fori_loop(0, blocks_dev, step, 0, unroll=unroll)

    def settle(row, carry):
        leave(row).wait()
        return carry

    lax.fori_loop(0, blocks_dev, settle, 0)


ROUND = ((0, 1), (1, 3), (3, 2), (2, 0))
ACROSS = ((0, 2), (2, 0), (1, 3), (3, 1))
FIRST_HOP = (
    ((1, 1), (3, 1)), ((3, 1), (3, 0)), ((3, 0), (1, 0)), ((1, 0), (1, 1)),
    ((2, 1), (0, 1)), ((0, 1), (0, 0)), ((0, 0), (2, 0)), ((2, 0), (2, 1)),
)
SECOND_HOP = (
    ((0, 1), (1, 1)), ((1, 1), (3, 0)), ((3, 0), (3, 1)), ((3, 1), (2, 1)), ((2, 1), (0, 0)), ((0, 0), (0, 1)),
    ((1, 0), (2, 0)), ((2, 0), (1, 0)),
)


def neighbours(count, first):
    pairs = [p for low in range(first, count - 1, 2) for p in ((low, low + 1), (low + 1, low))]
    return pairs, [place for place in range(count) if all(place != source for source, _ in pairs)]


def permuted(value, pairs):
    inner = lax.axis_size("gy")
    return lax.ppermute(value, ("gx", "gy"), sorted((a * inner + b, c * inner + d) for (a, b), (c, d) in pairs))


def along_x(line, pairs):
    return [((source, line), (target, line)) for source, target in pairs]


def along_y(line, pairs):
    return [((line, source), (line, target)) for source, target in pairs]


def x_swap(value, first):
    outer, inner = lax.axis_size("gx"), lax.axis_size("gy")
    pairs, alone = neighbours(outer, first)
    moves = [move for line in range(inner) for move in along_x(line, pairs)]
    moves += [move for place in alone for move in along_y(place, neighbours(inner, 0)[0])]
    return permuted(value, moves)


def by_corner():
    return lax.axis_size("gx") == 4 and lax.axis_size("gy") % 2 == 0


def hop(value, moves):
    lines = range(0, lax.axis_size("gy"), 2)
    return permuted(value, [((a, low + p), (c, low + q)) for low in lines for (a, p), (c, q) in moves])


def y_swap(value, first, idle=()):
    outer, inner = lax.axis_size("gx"), lax.axis_size("gy")
    pairs, alone = neighbours(inner, first)
    moves = [move for line in range(outer) for move in along_y(line, pairs)]
    if outer != 4:
        idle = neighbours(outer, 0)[0]
    return permuted(value, moves + [move for place in alone for move in along_x(place, idle)])


def local(labels, weights, column_index, send_index, seed_doc, seed_topic):
    blocks_dev, slots, block_size, _ = weights.shape
    documents = blocks_dev * block_size
    topics = labels.shape[1]
    sends = send_index.shape[2]
    seeds = seed_doc.shape[0]
    labels = unmoved(labels.reshape(blocks_dev, block_size, topics))
    weights = unmoved(weights)
    send_index = unmoved(send_index)
    seed_doc = seed_doc.reshape(1, seeds)
    seed_topic = seed_topic.reshape(1, seeds)
    whole = VMEM((sends, block_size, topics), jnp.bfloat16)
    held_shape = VMEM(weights.shape, jnp.bfloat16)
    extended_shape = VMEM((blocks_dev + 4 * sends, block_size, topics), jnp.bfloat16)
    scale_shape = VMEM((blocks_dev, block_size, block_size), jnp.float32)
    count_shape = VMEM((blocks_dev, block_size, topics), jnp.bfloat16)
    partial_shape = VMEM((blocks_dev, block_size, topics), jnp.float32)

    x_a, x_b, held, extended, scales, columns, lists = call(
        first_send_body,
        (whole, whole, held_shape, extended_shape, scale_shape)
        + (pltpu.SMEM((slots, blocks_dev), jnp.int32), pltpu.SMEM(send_index.shape, jnp.int32)),
        (IN_VMEM,) * 5 + (IN_SMEM,) * 2,
        (ANYWHERE,) * 4,
        (
            pltpu.VMEM((2 * sends + EARLY, block_size, topics), jnp.float32),
            pltpu.SMEM((blocks_dev,), jnp.int32),
            pltpu.SMEM((2 * sends,), jnp.int32),
            pltpu.SemaphoreType.DMA((2 * sends + EARLY, 2)),
            pltpu.SemaphoreType.DMA((2,)),
        ),
    )(unmoved(column_index.T), send_index, weights, labels)
    x_b = x_swap(x_b, 1)
    x_a = x_swap(x_a, 0)
    columns, lists = tabled(columns), tabled(lists)

    held, extended, scales, counts, y_a, y_b = call(
        functools.partial(degree_body, chunk=4),
        (held_shape, extended_shape, scale_shape, count_shape, whole, whole),
        (IN_VMEM,) * 6,
        (IN_SMEM,) + (IN_VMEM,) * 2 + (ANYWHERE,) * 2 + (IN_VMEM,) * 3,
        (
            pltpu.VMEM((blocks_dev, block_size, topics), jnp.float32),
            pltpu.VMEM((seeds, topics), jnp.bfloat16),
            pltpu.SMEM((blocks_dev,), jnp.int32),
            pltpu.SMEM((blocks_dev,), jnp.int32),
            pltpu.SemaphoreType.DMA((blocks_dev, 2)),
        ),
        aliases={5: 0, 6: 1, 7: 2},
    )(lists, seed_doc, seed_topic, weights, labels, pinned(held), pinned(extended), pinned(scales))
    y_a, y_b = y_swap(y_a, 0), y_swap(y_b, 1, ROUND)
    held, scales, counts = pinned(held), pinned(scales), pinned(counts)

    def started(extended, *reused):
        return call(
            functools.partial(near_body, unroll=16),
            partial_shape,
            IN_VMEM,
            (IN_SMEM,) + (IN_VMEM,) * (4 + len(reused)),
            aliases={4 + len(reused): 0} if reused else {},
        )(columns, held, pinned(extended), scales, counts, *reused)

    partial = started(extended)
    x_a, x_b, y_a, y_b, extended = call(
        second_send_body,
        (whole, whole, whole, whole, extended_shape),
        (IN_VMEM,) * 5,
        (IN_SMEM,) * 2 + (IN_VMEM,) * 8,
        aliases={3: 4},
    )(columns, lists, held, pinned(extended), scales, pinned(partial), *map(pinned, (x_b, x_a, y_b, y_a)))
    x_a = x_swap(x_a, 0)
    if by_corner():
        first_hop = hop(x_b, FIRST_HOP)
        x_b = call(hand_on_body, whole, IN_VMEM, (IN_VMEM,) * 2)(*map(pinned, (x_b, first_hop)))
        x_b = hop(x_b, SECOND_HOP)
    else:
        x_b = x_swap(x_b, 1)
    y_a, y_b = y_swap(y_a, 0), y_swap(y_b, 1)

    following, partial = call(
        functools.partial(rest_body, unroll=16),
        (extended_shape, partial_shape),
        (IN_VMEM,) * 2,
        (IN_SMEM,) + (IN_VMEM,) * 4,
        aliases={4: 1},
    )(columns, held, pinned(extended), scales, pinned(partial))
    partial = started(following, pinned(extended), pinned(partial))

    out, _ = call(
        functools.partial(last_body, unroll=16),
        (jax.ShapeDtypeStruct((blocks_dev, block_size, topics), jnp.float32), extended_shape),
        (ANYWHERE, IN_VMEM),
        (IN_SMEM,) + (IN_VMEM,) * 8,
        (
            pltpu.VMEM((blocks_dev, block_size, topics), jnp.float32),
            pltpu.SemaphoreType.DMA((blocks_dev,)),
        ),
        aliases={2: 1},
    )(columns, held, pinned(following), scales, pinned(partial), *map(pinned, (x_a, x_b, y_a, y_b)))
    return out.reshape(documents, topics)


def solution(mesh):
    in_specs = (
        P(("gx", "gy"), None),
        P(("gx", "gy"), None, None, None),
        P(("gx", "gy"), None),
        P(("gx", "gy"), None, None),
        P(("gx", "gy")),
        P(("gx", "gy")),
    )
    out_specs = P(("gx", "gy"), None)
    return jax.shard_map(local, mesh=mesh, in_specs=in_specs, out_specs=out_specs, check_vma=False)
```

```python
import functools

import jax
import jax.numpy as jnp
from jax import lax
from jax.experimental import pallas as pl
from jax.experimental.pallas import tpu as pltpu
from jax.sharding import PartitionSpec as P

ITERS = 2

ALPHA = 0.99
GAIN = 1.0 / (1.0 - 0.99)
SEED_WEIGHT = (1.0 - ALPHA) * GAIN

EARLY = 4
LOCAL = 8
VMEM = pltpu.VMEM
IN_VMEM = pl.BlockSpec(memory_space=pltpu.VMEM)
IN_SMEM = pl.BlockSpec(memory_space=pltpu.SMEM)
ANYWHERE = pl.BlockSpec(memory_space=pl.ANY)


def call(body, out_shape, out_specs, in_specs, scratch=(), aliases=None, limit=8):
    return pl.pallas_call(
        body,
        out_shape=out_shape,
        in_specs=in_specs,
        out_specs=out_specs,
        scratch_shapes=scratch,
        input_output_aliases=aliases or {},
        compiler_params=pltpu.CompilerParams(vmem_limit_bytes=limit * 2**20),
        cost_estimate=pl.CostEstimate(flops=1, bytes_accessed=1, transcendentals=0),
    )


def pinned(value):
    return pltpu.with_memory_space_constraint(value, pltpu.VMEM)


def unmoved(value):
    return pltpu.with_memory_space_constraint(value, pltpu.HBM)


def tabled(value):
    return pltpu.with_memory_space_constraint(value, pltpu.SMEM)


def row_scale(weights, row):
    slots = weights.shape[1]
    total = weights[row, 0].astype(jnp.float32)
    for slot in range(1, slots):
        total = total + weights[row, slot].astype(jnp.float32)
    return lax.rsqrt(jnp.sum(total, axis=1, keepdims=True))


def spread_over(scale, width):
    return jnp.concatenate([scale] * (width // scale.shape[1]), axis=1)


def toward_x():
    turn = lax.axis_index("gx") % 2
    return (3 - turn, 2 + turn)


def toward_y():
    turn = lax.axis_index("gy") % 2
    return (1 - turn, turn)


def sent_row(send_index, order, sends, i):
    return send_index[0, order[i // sends], i % sends]


def weighted(weights, extended, columns, row, first, last):
    left = jnp.concatenate([weights[row, slot] for slot in range(first, last)], axis=1)
    right = jnp.concatenate([extended[columns[slot, row]] for slot in range(first, last)], axis=0)
    return jnp.dot(left, right, preferred_element_type=jnp.float32)


def row_copies(weights, labels, held, block, sem, row, slot):
    return (
        pltpu.make_async_copy(weights.at[row], held.at[row], sem.at[slot, 0]),
        pltpu.make_async_copy(labels.at[row], block.at[slot], sem.at[slot, 1]),
    )


def scale_row(held, block, extended, scales, row, slot):
    scale = row_scale(held, row)
    scales[row] = jnp.broadcast_to(scale, scales.shape[1:])
    extended[row] = (scale * block[slot]).astype(jnp.bfloat16)


def copy_out(source, send_index, order, outs):
    sends = send_index.shape[2]
    i = 0
    for out in outs:
        for j in range(out.shape[0]):
            out[j] = source[sent_row(send_index, order, sends, i)]
            i += 1


def first_send_body(
    column_index, send_index, weights, labels, x_a, x_b, held, extended, scales, columns, lists,
    block, seen, fresh, sem, table_sem,
):
    blocks_dev = held.shape[0]
    get_lists = pltpu.make_async_copy(send_index, lists, table_sem.at[0])
    get_columns = pltpu.make_async_copy(column_index, columns, table_sem.at[1])
    get_lists.start()
    get_columns.start()

    def unseen(row, carry):
        seen[row] = 0
        return carry

    sends = x_a.shape[0]
    early = block.shape[0] - 2 * sends
    for row in range(early):
        for copy in row_copies(weights, labels, held, block, sem, row, 2 * sends + row):
            copy.start()
    lax.fori_loop(0, blocks_dev, unseen, 0, unroll=8)
    for row in range(early):
        seen[row] = 1
    get_lists.wait()
    order = toward_x()
    rows = [sent_row(lists, order, sends, i) for i in range(len(order) * sends)]
    for i, row in enumerate(rows):
        fresh[i] = 1 - seen[row]
        seen[row] = 1

        @pl.when(fresh[i] == 1)
        def _():
            for copy in row_copies(weights, labels, held, block, sem, row, i):
                copy.start()

    for row in range(early):
        for copy in row_copies(weights, labels, held, block, sem, row, 2 * sends + row):
            copy.wait()
    for row in range(early):
        scale_row(held, block, extended, scales, row, 2 * sends + row)
    for i, row in enumerate(rows):

        @pl.when(fresh[i] == 1)
        def _():
            for copy in row_copies(weights, labels, held, block, sem, row, i):
                copy.wait()
            scale_row(held, block, extended, scales, row, i)

        out = x_a if i < sends else x_b
        out[i % sends] = extended[row]
    get_columns.wait()


def degree_body(
    lists, seed_doc, seed_topic, weights, labels, held_in, extended_in, scales_in,
    held, extended, scales, counts, y_a, y_b, block, topic_hot, seen, left, sem, *, chunk,
):
    blocks_dev, block_size, topics = block.shape
    seeds = seed_doc.shape[1]

    def unseen(row, carry):
        seen[row] = 0
        return carry

    lax.fori_loop(0, blocks_dev, unseen, 0, unroll=8)
    for direction in toward_x():
        for i in range(lists.shape[2]):
            seen[lists[0, direction, i]] = 1
    for row in range(EARLY):
        seen[row] = 1

    def fetch(row, number):
        @pl.when(seen[row] == 0)
        def _():
            left[number] = row
            for copy in row_copies(weights, labels, held, block, sem, row, number):
                copy.start()

        return number + 1 - seen[row]

    number = lax.fori_loop(0, blocks_dev, fetch, jnp.int32(0))
    topic = lax.broadcasted_iota(jnp.int32, (topics, seeds), 0)
    hot = jnp.where(topic == seed_topic[...], 1.0, 0.0).astype(jnp.float32)
    topic_hot[...] = hot.T.astype(jnp.bfloat16)

    def count(row, carry):
        document = lax.broadcasted_iota(jnp.int32, (block_size, seeds), 0) + row * block_size
        doc_hot = jnp.where(document == seed_doc[...], 1.0, 0.0).astype(jnp.bfloat16)
        hits = jnp.dot(doc_hot, topic_hot[...], preferred_element_type=jnp.float32)
        counts[row] = hits.astype(jnp.bfloat16)
        return carry

    lax.fori_loop(0, blocks_dev, count, 0, unroll=8)

    def step(c, carry):
        slots = [jnp.minimum(c * chunk + i, number - 1) for i in range(chunk)]
        for i, slot in enumerate(slots):

            @pl.when(c * chunk + i < number)
            def _():
                for copy in row_copies(weights, labels, held, block, sem, left[slot], slot):
                    copy.wait()

        for slot in slots:
            scale_row(held, block, extended, scales, left[slot], slot)
        return carry

    lax.fori_loop(0, lax.div(number + chunk - 1, jnp.int32(chunk)), step, 0)
    copy_out(extended, lists, toward_y(), (y_a, y_b))


def pick_body(lists, source, out, *, number):
    direction = toward_y()[number]
    for i in range(out.shape[0]):
        out[i] = source[lists[0, direction, i]]


def near(weights, extended, columns, scales, counts, row):
    topics = extended.shape[2]
    product = weighted(weights, extended, columns, row, 0, LOCAL)
    return spread_over(ALPHA * scales[row], topics) * product + SEED_WEIGHT * counts[row].astype(jnp.float32)


def near_body(columns, weights, extended, scales, counts, *rest, unroll):
    partial = rest[-1]

    def step(row, carry):
        partial[row] = near(weights, extended, columns, scales, counts, row)
        return carry

    lax.fori_loop(0, partial.shape[0], step, 0, unroll=unroll)


def arrivals(pieces, extended):
    sends = pieces[0].shape[0]
    low = extended.shape[0] - 4 * sends
    order = toward_x() + toward_y()
    i = 0
    for piece in pieces:
        extended[pl.ds(low + order[i // sends] * sends + i % sends, piece.shape[0])] = piece[...]
        i += piece.shape[0]


def finished(weights, extended, columns, scales, partial, row):
    topics = partial.shape[2]
    slots = weights.shape[1]
    product = weighted(weights, extended, columns, row, LOCAL, slots)
    return partial[row] + spread_over(ALPHA * scales[row], topics) * product


def corner_send_body(columns, lists, weights, extended_in, scales, partial, r0, r1, r2, r3, x_b, extended):
    arrivals((r1, r0, r3, r2), extended)
    send(columns, lists, weights, extended, scales, partial, toward_x()[1], x_b)


def send_body(columns, lists, weights, extended, scales, partial, out, *, number):
    send(columns, lists, weights, extended, scales, partial, (toward_x() + toward_y())[number], out)


def y_send_body(columns, lists, weights, extended, scales, partial, y_a, y_b):
    for direction, out in zip(toward_y(), (y_a, y_b)):
        send(columns, lists, weights, extended, scales, partial, direction, out)


def send(columns, lists, weights, extended, scales, partial, direction, out):
    for i in range(out.shape[0]):
        row = lists[0, direction, i]
        value = finished(weights, extended, columns, scales, partial, row)
        out[i] = (spread_over(scales[row], out.shape[2]) * value).astype(jnp.bfloat16)


def rest_body(columns, weights, extended, scales, partial, following, handed, *, unroll):
    blocks_dev, _, topics = partial.shape

    def finish(row, carry):
        value = finished(weights, extended, columns, scales, partial, row)
        following[row] = (spread_over(scales[row], topics) * value).astype(jnp.bfloat16)
        return carry

    lax.fori_loop(0, blocks_dev, finish, 0, unroll=unroll)


def hand_on_body(direct, first_hop, out):
    straight = lax.axis_index("gy") % 2 == 0

    @pl.when(straight)
    def _():
        out[...] = direct[...]

    @pl.when(jnp.logical_not(straight))
    def _():
        out[...] = first_hop[...]


def last_body(
    columns, weights, extended_in, scales, partial, r0, r1, r2, r3, out, extended, block, sem, *, unroll
):
    blocks_dev = partial.shape[0]
    arrivals((r0, r1, r2, r3), extended)

    def leave(row):
        return pltpu.make_async_copy(block.at[row], out.at[row], sem.at[row])

    def step(row, carry):
        block[row] = finished(weights, extended, columns, scales, partial, row)
        leave(row).start()
        return carry

    lax.fori_loop(0, blocks_dev, step, 0, unroll=unroll)

    def settle(row, carry):
        leave(row).wait()
        return carry

    lax.fori_loop(0, blocks_dev, settle, 0)


ROUND = ((0, 1), (1, 3), (3, 2), (2, 0))
ACROSS = ((0, 2), (2, 0), (1, 3), (3, 1))
FIRST_HOP = (
    ((1, 1), (3, 1)), ((3, 1), (3, 0)), ((3, 0), (1, 0)), ((1, 0), (1, 1)),
    ((2, 1), (0, 1)), ((0, 1), (0, 0)), ((0, 0), (2, 0)), ((2, 0), (2, 1)),
)
SECOND_HOP = (
    ((0, 1), (1, 1)), ((1, 1), (3, 0)), ((3, 0), (3, 1)), ((3, 1), (2, 1)), ((2, 1), (0, 0)), ((0, 0), (0, 1)),
    ((1, 0), (2, 0)), ((2, 0), (1, 0)),
)


def neighbours(count, first):
    pairs = [p for low in range(first, count - 1, 2) for p in ((low, low + 1), (low + 1, low))]
    return pairs, [place for place in range(count) if all(place != source for source, _ in pairs)]


def permuted(value, pairs):
    inner = lax.axis_size("gy")
    return lax.ppermute(value, ("gx", "gy"), sorted((a * inner + b, c * inner + d) for (a, b), (c, d) in pairs))


def along_x(line, pairs):
    return [((source, line), (target, line)) for source, target in pairs]


def along_y(line, pairs):
    return [((line, source), (line, target)) for source, target in pairs]


def x_swap(value, first):
    outer, inner = lax.axis_size("gx"), lax.axis_size("gy")
    pairs, alone = neighbours(outer, first)
    moves = [move for line in range(inner) for move in along_x(line, pairs)]
    moves += [move for place in alone for move in along_y(place, neighbours(inner, 0)[0])]
    return permuted(value, moves)


def by_corner():
    return lax.axis_size("gx") == 4 and lax.axis_size("gy") % 2 == 0


def hop(value, moves):
    lines = range(0, lax.axis_size("gy"), 2)
    return permuted(value, [((a, low + p), (c, low + q)) for low in lines for (a, p), (c, q) in moves])


def y_swap(value, first, idle=()):
    outer, inner = lax.axis_size("gx"), lax.axis_size("gy")
    pairs, alone = neighbours(inner, first)
    moves = [move for line in range(outer) for move in along_y(line, pairs)]
    if outer != 4:
        idle = neighbours(outer, 0)[0]
    return permuted(value, moves + [move for place in alone for move in along_x(place, idle)])


def local(labels, weights, column_index, send_index, seed_doc, seed_topic):
    blocks_dev, slots, block_size, _ = weights.shape
    documents = blocks_dev * block_size
    topics = labels.shape[1]
    sends = send_index.shape[2]
    seeds = seed_doc.shape[0]
    labels = unmoved(labels.reshape(blocks_dev, block_size, topics))
    weights = unmoved(weights)
    send_index = unmoved(send_index)
    seed_doc = seed_doc.reshape(1, seeds)
    seed_topic = seed_topic.reshape(1, seeds)
    whole = VMEM((sends, block_size, topics), jnp.bfloat16)
    held_shape = VMEM(weights.shape, jnp.bfloat16)
    extended_shape = VMEM((blocks_dev + 4 * sends, block_size, topics), jnp.bfloat16)
    scale_shape = VMEM((blocks_dev, block_size, block_size), jnp.float32)
    count_shape = VMEM((blocks_dev, block_size, topics), jnp.bfloat16)
    partial_shape = VMEM((blocks_dev, block_size, topics), jnp.float32)

    x_a, x_b, held, extended, scales, columns, lists = call(
        first_send_body,
        (whole, whole, held_shape, extended_shape, scale_shape)
        + (pltpu.SMEM((slots, blocks_dev), jnp.int32), pltpu.SMEM(send_index.shape, jnp.int32)),
        (IN_VMEM,) * 5 + (IN_SMEM,) * 2,
        (ANYWHERE,) * 4,
        (
            pltpu.VMEM((2 * sends + EARLY, block_size, topics), jnp.float32),
            pltpu.SMEM((blocks_dev,), jnp.int32),
            pltpu.SMEM((2 * sends,), jnp.int32),
            pltpu.SemaphoreType.DMA((2 * sends + EARLY, 2)),
            pltpu.SemaphoreType.DMA((2,)),
        ),
    )(unmoved(column_index.T), send_index, weights, labels)
    x_b = x_swap(x_b, 1)
    x_a = x_swap(x_a, 0)
    columns, lists = tabled(columns), tabled(lists)

    held, extended, scales, counts, y_a, y_b = call(
        functools.partial(degree_body, chunk=4),
        (held_shape, extended_shape, scale_shape, count_shape, whole, whole),
        (IN_VMEM,) * 6,
        (IN_SMEM,) + (IN_VMEM,) * 2 + (ANYWHERE,) * 2 + (IN_VMEM,) * 3,
        (
            pltpu.VMEM((blocks_dev, block_size, topics), jnp.float32),
            pltpu.VMEM((seeds, topics), jnp.bfloat16),
            pltpu.SMEM((blocks_dev,), jnp.int32),
            pltpu.SMEM((blocks_dev,), jnp.int32),
            pltpu.SemaphoreType.DMA((blocks_dev, 2)),
        ),
        aliases={5: 0, 6: 1, 7: 2},
    )(lists, seed_doc, seed_topic, weights, labels, pinned(held), pinned(extended), pinned(scales))
    y_a, y_b = y_swap(y_a, 0), y_swap(y_b, 1, ROUND)
    held, scales, counts = pinned(held), pinned(scales), pinned(counts)

    def started(extended, *reused):
        return call(
            functools.partial(near_body, unroll=16),
            partial_shape,
            IN_VMEM,
            (IN_SMEM,) + (IN_VMEM,) * (4 + len(reused)),
            aliases={4 + len(reused): 0} if reused else {},
        )(columns, held, pinned(extended), scales, counts, *reused)

    partial = started(extended)
    x_b, extended = call(
        corner_send_body,
        (whole, extended_shape),
        (IN_VMEM,) * 2,
        (IN_SMEM,) * 2 + (IN_VMEM,) * 8,
        aliases={3: 1},
    )(columns, lists, held, pinned(extended), scales, pinned(partial), *map(pinned, (x_b, x_a, y_b, y_a)))
    x_a = call(functools.partial(send_body, number=0), whole, IN_VMEM, (IN_SMEM,) * 2 + (IN_VMEM,) * 4)(
        columns, lists, held, pinned(extended), scales, pinned(partial)
    )
    y_a, y_b = call(y_send_body, (whole, whole), (IN_VMEM,) * 2, (IN_SMEM,) * 2 + (IN_VMEM,) * 4)(
        columns, lists, held, pinned(extended), scales, pinned(partial)
    )
    x_a = x_swap(x_a, 0)
    if by_corner():
        first_hop = hop(x_b, FIRST_HOP)
        x_b = call(hand_on_body, whole, IN_VMEM, (IN_VMEM,) * 2)(*map(pinned, (x_b, first_hop)))
        x_b = hop(x_b, SECOND_HOP)
    else:
        x_b = x_swap(x_b, 1)
    y_a, y_b = y_swap(y_a, 0), y_swap(y_b, 1)

    following, partial = call(
        functools.partial(rest_body, unroll=16),
        (extended_shape, partial_shape),
        (IN_VMEM,) * 2,
        (IN_SMEM,) + (IN_VMEM,) * 4,
        aliases={4: 1},
    )(columns, held, pinned(extended), scales, pinned(partial))
    partial = started(following, pinned(extended), pinned(partial))

    out, _ = call(
        functools.partial(last_body, unroll=16),
        (jax.ShapeDtypeStruct((blocks_dev, block_size, topics), jnp.float32), extended_shape),
        (ANYWHERE, IN_VMEM),
        (IN_SMEM,) + (IN_VMEM,) * 8,
        (
            pltpu.VMEM((blocks_dev, block_size, topics), jnp.float32),
            pltpu.SemaphoreType.DMA((blocks_dev,)),
        ),
        aliases={2: 1},
    )(columns, held, pinned(following), scales, pinned(partial), *map(pinned, (x_a, x_b, y_a, y_b)))
    return out.reshape(documents, topics)


def solution(mesh):
    in_specs = (
        P(("gx", "gy"), None),
        P(("gx", "gy"), None, None, None),
        P(("gx", "gy"), None),
        P(("gx", "gy"), None, None),
        P(("gx", "gy")),
        P(("gx", "gy")),
    )
    out_specs = P(("gx", "gy"), None)
    return jax.shard_map(local, mesh=mesh, in_specs=in_specs, out_specs=out_specs, check_vma=False)
```

```python
import functools

import jax
import jax.numpy as jnp
from jax import lax
from jax.experimental import pallas as pl
from jax.experimental.pallas import tpu as pltpu
from jax.sharding import PartitionSpec as P

ITERS = 2

ALPHA = 0.99
GAIN = 1.0 / (1.0 - 0.99)
SEED_WEIGHT = (1.0 - ALPHA) * GAIN

EARLY = 4
LOCAL = 8
VMEM = pltpu.VMEM
IN_VMEM = pl.BlockSpec(memory_space=pltpu.VMEM)
IN_SMEM = pl.BlockSpec(memory_space=pltpu.SMEM)
ANYWHERE = pl.BlockSpec(memory_space=pl.ANY)


def call(body, out_shape, out_specs, in_specs, scratch=(), aliases=None, limit=8):
    return pl.pallas_call(
        body,
        out_shape=out_shape,
        in_specs=in_specs,
        out_specs=out_specs,
        scratch_shapes=scratch,
        input_output_aliases=aliases or {},
        compiler_params=pltpu.CompilerParams(vmem_limit_bytes=limit * 2**20),
        cost_estimate=pl.CostEstimate(flops=1, bytes_accessed=1, transcendentals=0),
    )


def pinned(value):
    return pltpu.with_memory_space_constraint(value, pltpu.VMEM)


def unmoved(value):
    return pltpu.with_memory_space_constraint(value, pltpu.HBM)


def tabled(value):
    return pltpu.with_memory_space_constraint(value, pltpu.SMEM)


def row_scale(weights, row):
    slots = weights.shape[1]
    total = weights[row, 0].astype(jnp.float32)
    for slot in range(1, slots):
        total = total + weights[row, slot].astype(jnp.float32)
    return lax.rsqrt(jnp.sum(total, axis=1, keepdims=True))


def spread_over(scale, width):
    return jnp.concatenate([scale] * (width // scale.shape[1]), axis=1)


def toward_x():
    turn = lax.axis_index("gx") % 2
    return (3 - turn, 2 + turn)


def toward_y():
    turn = lax.axis_index("gy") % 2
    return (1 - turn, turn)


def sent_row(send_index, order, sends, i):
    return send_index[0, order[i // sends], i % sends]


def weighted(weights, extended, columns, row, first, last):
    left = jnp.concatenate([weights[row, slot] for slot in range(first, last)], axis=1)
    right = jnp.concatenate([extended[columns[slot, row]] for slot in range(first, last)], axis=0)
    return jnp.dot(left, right, preferred_element_type=jnp.float32)


def row_copies(weights, labels, held, block, sem, row, slot):
    return (
        pltpu.make_async_copy(weights.at[row], held.at[row], sem.at[slot, 0]),
        pltpu.make_async_copy(labels.at[row], block.at[slot], sem.at[slot, 1]),
    )


def scale_row(held, block, extended, scales, row, slot):
    scale = row_scale(held, row)
    scales[row] = jnp.broadcast_to(scale, scales.shape[1:])
    extended[row] = (scale * block[slot]).astype(jnp.bfloat16)


def copy_out(source, send_index, order, outs):
    sends = send_index.shape[2]
    i = 0
    for out in outs:
        for j in range(out.shape[0]):
            out[j] = source[sent_row(send_index, order, sends, i)]
            i += 1


def first_send_body(
    column_index, send_index, weights, labels, x_a, x_b, held, extended, scales, columns, lists,
    block, seen, fresh, sem, table_sem,
):
    blocks_dev = held.shape[0]
    get_lists = pltpu.make_async_copy(send_index, lists, table_sem.at[0])
    get_columns = pltpu.make_async_copy(column_index, columns, table_sem.at[1])
    get_lists.start()
    get_columns.start()

    def unseen(row, carry):
        seen[row] = 0
        return carry

    sends = x_a.shape[0]
    early = block.shape[0] - 2 * sends
    for row in range(early):
        for copy in row_copies(weights, labels, held, block, sem, row, 2 * sends + row):
            copy.start()
    lax.fori_loop(0, blocks_dev, unseen, 0, unroll=8)
    for row in range(early):
        seen[row] = 1
    get_lists.wait()
    order = toward_x()
    rows = [sent_row(lists, order, sends, i) for i in range(len(order) * sends)]
    for i, row in enumerate(rows):
        fresh[i] = 1 - seen[row]
        seen[row] = 1

        @pl.when(fresh[i] == 1)
        def _():
            for copy in row_copies(weights, labels, held, block, sem, row, i):
                copy.start()

    for row in range(early):
        for copy in row_copies(weights, labels, held, block, sem, row, 2 * sends + row):
            copy.wait()
    for row in range(early):
        scale_row(held, block, extended, scales, row, 2 * sends + row)
    for i, row in enumerate(rows):

        @pl.when(fresh[i] == 1)
        def _():
            for copy in row_copies(weights, labels, held, block, sem, row, i):
                copy.wait()
            scale_row(held, block, extended, scales, row, i)

        out = x_a if i < sends else x_b
        out[i % sends] = extended[row]
    get_columns.wait()


def degree_body(
    lists, seed_doc, seed_topic, weights, labels, held_in, extended_in, scales_in,
    held, extended, scales, counts, y_a, y_b, block, topic_hot, seen, left, sem, *, chunk,
):
    blocks_dev, block_size, topics = block.shape
    seeds = seed_doc.shape[1]

    def unseen(row, carry):
        seen[row] = 0
        return carry

    lax.fori_loop(0, blocks_dev, unseen, 0, unroll=8)
    for direction in toward_x():
        for i in range(lists.shape[2]):
            seen[lists[0, direction, i]] = 1
    for row in range(EARLY):
        seen[row] = 1

    def fetch(row, number):
        @pl.when(seen[row] == 0)
        def _():
            left[number] = row
            for copy in row_copies(weights, labels, held, block, sem, row, number):
                copy.start()

        return number + 1 - seen[row]

    number = lax.fori_loop(0, blocks_dev, fetch, jnp.int32(0))
    topic = lax.broadcasted_iota(jnp.int32, (topics, seeds), 0)
    hot = jnp.where(topic == seed_topic[...], 1.0, 0.0).astype(jnp.float32)
    topic_hot[...] = hot.T.astype(jnp.bfloat16)

    def count(row, carry):
        document = lax.broadcasted_iota(jnp.int32, (block_size, seeds), 0) + row * block_size
        doc_hot = jnp.where(document == seed_doc[...], 1.0, 0.0).astype(jnp.bfloat16)
        hits = jnp.dot(doc_hot, topic_hot[...], preferred_element_type=jnp.float32)
        counts[row] = hits.astype(jnp.bfloat16)
        return carry

    lax.fori_loop(0, blocks_dev, count, 0, unroll=8)

    def step(c, carry):
        slots = [jnp.minimum(c * chunk + i, number - 1) for i in range(chunk)]
        for i, slot in enumerate(slots):

            @pl.when(c * chunk + i < number)
            def _():
                for copy in row_copies(weights, labels, held, block, sem, left[slot], slot):
                    copy.wait()

        for slot in slots:
            scale_row(held, block, extended, scales, left[slot], slot)
        return carry

    lax.fori_loop(0, lax.div(number + chunk - 1, jnp.int32(chunk)), step, 0)
    copy_out(extended, lists, toward_y(), (y_a, y_b))


def pick_body(lists, source, out, *, number):
    direction = toward_y()[number]
    for i in range(out.shape[0]):
        out[i] = source[lists[0, direction, i]]


def near(weights, extended, columns, scales, counts, row):
    topics = extended.shape[2]
    product = weighted(weights, extended, columns, row, 0, LOCAL)
    return spread_over(ALPHA * scales[row], topics) * product + SEED_WEIGHT * counts[row].astype(jnp.float32)


def near_body(columns, weights, extended, scales, counts, *rest, unroll):
    partial = rest[-1]

    def step(row, carry):
        partial[row] = near(weights, extended, columns, scales, counts, row)
        return carry

    lax.fori_loop(0, partial.shape[0], step, 0, unroll=unroll)


def arrivals(pieces, extended):
    sends = pieces[0].shape[0]
    low = extended.shape[0] - 4 * sends
    order = toward_x() + toward_y()
    i = 0
    for piece in pieces:
        extended[pl.ds(low + order[i // sends] * sends + i % sends, piece.shape[0])] = piece[...]
        i += piece.shape[0]


def finished(weights, extended, columns, scales, partial, row):
    topics = partial.shape[2]
    slots = weights.shape[1]
    product = weighted(weights, extended, columns, row, LOCAL, slots)
    return partial[row] + spread_over(ALPHA * scales[row], topics) * product


def corner_send_body(columns, lists, weights, extended_in, scales, partial, r0, r1, r2, r3, x_b, extended):
    arrivals((r1, r0, r3, r2), extended)
    send(columns, lists, weights, extended, scales, partial, toward_x()[1], x_b)


def send_body(columns, lists, weights, extended, scales, partial, out, *, number):
    send(columns, lists, weights, extended, scales, partial, (toward_x() + toward_y())[number], out)


def y_send_body(columns, lists, weights, extended, scales, partial, behind, y_a, y_b):
    for direction, out in zip(toward_y(), (y_a, y_b)):
        send(columns, lists, weights, extended, scales, partial, direction, out)


def send(columns, lists, weights, extended, scales, partial, direction, out):
    for i in range(out.shape[0]):
        row = lists[0, direction, i]
        value = finished(weights, extended, columns, scales, partial, row)
        out[i] = (spread_over(scales[row], out.shape[2]) * value).astype(jnp.bfloat16)


def rest_body(columns, weights, extended, scales, partial, following, handed, *, unroll):
    blocks_dev, _, topics = partial.shape

    def finish(row, carry):
        value = finished(weights, extended, columns, scales, partial, row)
        following[row] = (spread_over(scales[row], topics) * value).astype(jnp.bfloat16)
        return carry

    lax.fori_loop(0, blocks_dev, finish, 0, unroll=unroll)


def hand_on_body(direct, first_hop, out):
    straight = lax.axis_index("gy") % 2 == 0

    @pl.when(straight)
    def _():
        out[...] = direct[...]

    @pl.when(jnp.logical_not(straight))
    def _():
        out[...] = first_hop[...]


def last_body(
    columns, weights, extended_in, scales, partial, r0, r1, r2, r3, out, extended, block, sem, *, unroll
):
    blocks_dev = partial.shape[0]
    arrivals((r0, r1, r2, r3), extended)

    def leave(row):
        return pltpu.make_async_copy(block.at[row], out.at[row], sem.at[row])

    def step(row, carry):
        block[row] = finished(weights, extended, columns, scales, partial, row)
        leave(row).start()
        return carry

    lax.fori_loop(0, blocks_dev, step, 0, unroll=unroll)

    def settle(row, carry):
        leave(row).wait()
        return carry

    lax.fori_loop(0, blocks_dev, settle, 0)


ROUND = ((0, 1), (1, 3), (3, 2), (2, 0))
ACROSS = ((0, 2), (2, 0), (1, 3), (3, 1))
FIRST_HOP = (
    ((1, 1), (3, 1)), ((3, 1), (3, 0)), ((3, 0), (1, 0)), ((1, 0), (1, 1)),
    ((2, 1), (0, 1)), ((0, 1), (0, 0)), ((0, 0), (2, 0)), ((2, 0), (2, 1)),
)
SECOND_HOP = (
    ((0, 1), (1, 1)), ((1, 1), (3, 0)), ((3, 0), (3, 1)), ((3, 1), (2, 1)), ((2, 1), (0, 0)), ((0, 0), (0, 1)),
    ((1, 0), (2, 0)), ((2, 0), (1, 0)),
)


def neighbours(count, first):
    pairs = [p for low in range(first, count - 1, 2) for p in ((low, low + 1), (low + 1, low))]
    return pairs, [place for place in range(count) if all(place != source for source, _ in pairs)]


def permuted(value, pairs):
    inner = lax.axis_size("gy")
    return lax.ppermute(value, ("gx", "gy"), sorted((a * inner + b, c * inner + d) for (a, b), (c, d) in pairs))


def along_x(line, pairs):
    return [((source, line), (target, line)) for source, target in pairs]


def along_y(line, pairs):
    return [((line, source), (line, target)) for source, target in pairs]


def x_swap(value, first):
    outer, inner = lax.axis_size("gx"), lax.axis_size("gy")
    pairs, alone = neighbours(outer, first)
    moves = [move for line in range(inner) for move in along_x(line, pairs)]
    moves += [move for place in alone for move in along_y(place, neighbours(inner, 0)[0])]
    return permuted(value, moves)


def by_corner():
    return lax.axis_size("gx") == 4 and lax.axis_size("gy") % 2 == 0


def hop(value, moves):
    lines = range(0, lax.axis_size("gy"), 2)
    return permuted(value, [((a, low + p), (c, low + q)) for low in lines for (a, p), (c, q) in moves])


def y_swap(value, first, idle=()):
    outer, inner = lax.axis_size("gx"), lax.axis_size("gy")
    pairs, alone = neighbours(inner, first)
    moves = [move for line in range(outer) for move in along_y(line, pairs)]
    if outer != 4:
        idle = neighbours(outer, 0)[0]
    return permuted(value, moves + [move for place in alone for move in along_x(place, idle)])


def local(labels, weights, column_index, send_index, seed_doc, seed_topic):
    blocks_dev, slots, block_size, _ = weights.shape
    documents = blocks_dev * block_size
    topics = labels.shape[1]
    sends = send_index.shape[2]
    seeds = seed_doc.shape[0]
    labels = unmoved(labels.reshape(blocks_dev, block_size, topics))
    weights = unmoved(weights)
    send_index = unmoved(send_index)
    seed_doc = seed_doc.reshape(1, seeds)
    seed_topic = seed_topic.reshape(1, seeds)
    whole = VMEM((sends, block_size, topics), jnp.bfloat16)
    held_shape = VMEM(weights.shape, jnp.bfloat16)
    extended_shape = VMEM((blocks_dev + 4 * sends, block_size, topics), jnp.bfloat16)
    scale_shape = VMEM((blocks_dev, block_size, block_size), jnp.float32)
    count_shape = VMEM((blocks_dev, block_size, topics), jnp.bfloat16)
    partial_shape = VMEM((blocks_dev, block_size, topics), jnp.float32)

    x_a, x_b, held, extended, scales, columns, lists = call(
        first_send_body,
        (whole, whole, held_shape, extended_shape, scale_shape)
        + (pltpu.SMEM((slots, blocks_dev), jnp.int32), pltpu.SMEM(send_index.shape, jnp.int32)),
        (IN_VMEM,) * 5 + (IN_SMEM,) * 2,
        (ANYWHERE,) * 4,
        (
            pltpu.VMEM((2 * sends + EARLY, block_size, topics), jnp.float32),
            pltpu.SMEM((blocks_dev,), jnp.int32),
            pltpu.SMEM((2 * sends,), jnp.int32),
            pltpu.SemaphoreType.DMA((2 * sends + EARLY, 2)),
            pltpu.SemaphoreType.DMA((2,)),
        ),
    )(unmoved(column_index.T), send_index, weights, labels)
    x_b = x_swap(x_b, 1)
    x_a = x_swap(x_a, 0)
    columns, lists = tabled(columns), tabled(lists)

    held, extended, scales, counts, y_a, y_b = call(
        functools.partial(degree_body, chunk=4),
        (held_shape, extended_shape, scale_shape, count_shape, whole, whole),
        (IN_VMEM,) * 6,
        (IN_SMEM,) + (IN_VMEM,) * 2 + (ANYWHERE,) * 2 + (IN_VMEM,) * 3,
        (
            pltpu.VMEM((blocks_dev, block_size, topics), jnp.float32),
            pltpu.VMEM((seeds, topics), jnp.bfloat16),
            pltpu.SMEM((blocks_dev,), jnp.int32),
            pltpu.SMEM((blocks_dev,), jnp.int32),
            pltpu.SemaphoreType.DMA((blocks_dev, 2)),
        ),
        aliases={5: 0, 6: 1, 7: 2},
    )(lists, seed_doc, seed_topic, weights, labels, pinned(held), pinned(extended), pinned(scales))
    y_a, y_b = y_swap(y_a, 0), y_swap(y_b, 1, ROUND)
    held, scales, counts = pinned(held), pinned(scales), pinned(counts)

    def started(extended, *reused):
        return call(
            functools.partial(near_body, unroll=16),
            partial_shape,
            IN_VMEM,
            (IN_SMEM,) + (IN_VMEM,) * (4 + len(reused)),
            aliases={4 + len(reused): 0} if reused else {},
        )(columns, held, pinned(extended), scales, counts, *reused)

    partial = started(extended)
    x_b, extended = call(
        corner_send_body,
        (whole, extended_shape),
        (IN_VMEM,) * 2,
        (IN_SMEM,) * 2 + (IN_VMEM,) * 8,
        aliases={3: 1},
    )(columns, lists, held, pinned(extended), scales, pinned(partial), *map(pinned, (x_b, x_a, y_b, y_a)))
    x_a = call(functools.partial(send_body, number=0), whole, IN_VMEM, (IN_SMEM,) * 2 + (IN_VMEM,) * 4)(
        columns, lists, held, pinned(extended), scales, pinned(partial)
    )
    y_a, y_b = call(y_send_body, (whole, whole), (IN_VMEM,) * 2, (IN_SMEM,) * 2 + (IN_VMEM,) * 5)(
        columns, lists, held, pinned(extended), scales, pinned(partial), pinned(x_a)
    )
    x_a = x_swap(x_a, 0)
    if by_corner():
        first_hop = hop(x_b, FIRST_HOP)
        x_b = call(hand_on_body, whole, IN_VMEM, (IN_VMEM,) * 2)(*map(pinned, (x_b, first_hop)))
        x_b = hop(x_b, SECOND_HOP)
    else:
        x_b = x_swap(x_b, 1)
    y_a, y_b = y_swap(y_a, 0), y_swap(y_b, 1)

    following, partial = call(
        functools.partial(rest_body, unroll=16),
        (extended_shape, partial_shape),
        (IN_VMEM,) * 2,
        (IN_SMEM,) + (IN_VMEM,) * 4,
        aliases={4: 1},
    )(columns, held, pinned(extended), scales, pinned(partial))
    partial = started(following, pinned(extended), pinned(partial))

    out, _ = call(
        functools.partial(last_body, unroll=32),
        (jax.ShapeDtypeStruct((blocks_dev, block_size, topics), jnp.float32), extended_shape),
        (ANYWHERE, IN_VMEM),
        (IN_SMEM,) + (IN_VMEM,) * 8,
        (
            pltpu.VMEM((blocks_dev, block_size, topics), jnp.float32),
            pltpu.SemaphoreType.DMA((blocks_dev,)),
        ),
        aliases={2: 1},
    )(columns, held, pinned(following), scales, pinned(partial), *map(pinned, (x_a, x_b, y_a, y_b)))
    return out.reshape(documents, topics)


def solution(mesh):
    in_specs = (
        P(("gx", "gy"), None),
        P(("gx", "gy"), None, None, None),
        P(("gx", "gy"), None),
        P(("gx", "gy"), None, None),
        P(("gx", "gy")),
        P(("gx", "gy")),
    )
    out_specs = P(("gx", "gy"), None)
    return jax.shard_map(local, mesh=mesh, in_specs=in_specs, out_specs=out_specs, check_vma=False)
```

```python
import functools

import jax
import jax.numpy as jnp
from jax import lax
from jax.experimental import pallas as pl
from jax.experimental.pallas import tpu as pltpu
from jax.sharding import PartitionSpec as P

ITERS = 2

ALPHA = 0.99
GAIN = 1.0 / (1.0 - 0.99)
SEED_WEIGHT = (1.0 - ALPHA) * GAIN

EARLY = 2
LOCAL = 8
VMEM = pltpu.VMEM
IN_VMEM = pl.BlockSpec(memory_space=pltpu.VMEM)
IN_SMEM = pl.BlockSpec(memory_space=pltpu.SMEM)
ANYWHERE = pl.BlockSpec(memory_space=pl.ANY)


def call(body, out_shape, out_specs, in_specs, scratch=(), aliases=None, limit=8):
    return pl.pallas_call(
        body,
        out_shape=out_shape,
        in_specs=in_specs,
        out_specs=out_specs,
        scratch_shapes=scratch,
        input_output_aliases=aliases or {},
        compiler_params=pltpu.CompilerParams(vmem_limit_bytes=limit * 2**20),
        cost_estimate=pl.CostEstimate(flops=1, bytes_accessed=1, transcendentals=0),
    )


def pinned(value):
    return pltpu.with_memory_space_constraint(value, pltpu.VMEM)


def unmoved(value):
    return pltpu.with_memory_space_constraint(value, pltpu.HBM)


def tabled(value):
    return pltpu.with_memory_space_constraint(value, pltpu.SMEM)


def row_scale(weights, row):
    slots = weights.shape[1]
    total = weights[row, 0].astype(jnp.float32)
    for slot in range(1, slots):
        total = total + weights[row, slot].astype(jnp.float32)
    return lax.rsqrt(jnp.sum(total, axis=1, keepdims=True))


def spread_over(scale, width):
    return jnp.concatenate([scale] * (width // scale.shape[1]), axis=1)


def toward_x():
    turn = lax.axis_index("gx") % 2
    return (3 - turn, 2 + turn)


def toward_y():
    turn = lax.axis_index("gy") % 2
    return (1 - turn, turn)


def sent_row(send_index, order, sends, i):
    return send_index[0, order[i // sends], i % sends]


def weighted(weights, extended, columns, row, first, last):
    left = jnp.concatenate([weights[row, slot] for slot in range(first, last)], axis=1)
    right = jnp.concatenate([extended[columns[slot, row]] for slot in range(first, last)], axis=0)
    return jnp.dot(left, right, preferred_element_type=jnp.float32)


def row_copies(weights, labels, held, block, sem, row, slot):
    return (
        pltpu.make_async_copy(weights.at[row], held.at[row], sem.at[slot, 0]),
        pltpu.make_async_copy(labels.at[row], block.at[slot], sem.at[slot, 1]),
    )


def scale_row(held, block, extended, scales, row, slot):
    scale = row_scale(held, row)
    scales[row] = jnp.broadcast_to(scale, scales.shape[1:])
    extended[row] = (scale * block[slot]).astype(jnp.bfloat16)


def copy_out(source, send_index, order, outs):
    sends = send_index.shape[2]
    i = 0
    for out in outs:
        for j in range(out.shape[0]):
            out[j] = source[sent_row(send_index, order, sends, i)]
            i += 1


def first_send_body(
    column_index, send_index, weights, labels, x_a, x_b, held, extended, scales, columns, lists,
    block, seen, fresh, sem, table_sem,
):
    blocks_dev = held.shape[0]
    get_lists = pltpu.make_async_copy(send_index, lists, table_sem.at[0])
    get_columns = pltpu.make_async_copy(column_index, columns, table_sem.at[1])
    get_lists.start()
    get_columns.start()

    def unseen(row, carry):
        seen[row] = 0
        return carry

    sends = x_a.shape[0]
    early = block.shape[0] - 2 * sends
    for row in range(early):
        for copy in row_copies(weights, labels, held, block, sem, row, 2 * sends + row):
            copy.start()
    lax.fori_loop(0, blocks_dev, unseen, 0, unroll=8)
    for row in range(early):
        seen[row] = 1
    get_lists.wait()
    order = toward_x()
    rows = [sent_row(lists, order, sends, i) for i in range(len(order) * sends)]
    for i, row in enumerate(rows):
        fresh[i] = 1 - seen[row]
        seen[row] = 1

        @pl.when(fresh[i] == 1)
        def _():
            for copy in row_copies(weights, labels, held, block, sem, row, i):
                copy.start()

    for row in range(early):
        for copy in row_copies(weights, labels, held, block, sem, row, 2 * sends + row):
            copy.wait()
    for row in range(early):
        scale_row(held, block, extended, scales, row, 2 * sends + row)
    for i, row in enumerate(rows):

        @pl.when(fresh[i] == 1)
        def _():
            for copy in row_copies(weights, labels, held, block, sem, row, i):
                copy.wait()
            scale_row(held, block, extended, scales, row, i)

        out = x_a if i < sends else x_b
        out[i % sends] = extended[row]
    get_columns.wait()


def degree_body(
    lists, seed_doc, seed_topic, weights, labels, held_in, extended_in, scales_in,
    held, extended, scales, counts, y_a, y_b, block, topic_hot, seen, left, sem, *, chunk,
):
    blocks_dev, block_size, topics = block.shape
    seeds = seed_doc.shape[1]

    def unseen(row, carry):
        seen[row] = 0
        return carry

    lax.fori_loop(0, blocks_dev, unseen, 0, unroll=8)
    for direction in toward_x():
        for i in range(lists.shape[2]):
            seen[lists[0, direction, i]] = 1
    for row in range(EARLY):
        seen[row] = 1

    def fetch(row, number):
        @pl.when(seen[row] == 0)
        def _():
            left[number] = row
            for copy in row_copies(weights, labels, held, block, sem, row, number):
                copy.start()

        return number + 1 - seen[row]

    number = lax.fori_loop(0, blocks_dev, fetch, jnp.int32(0))
    topic = lax.broadcasted_iota(jnp.int32, (topics, seeds), 0)
    hot = jnp.where(topic == seed_topic[...], 1.0, 0.0).astype(jnp.float32)
    topic_hot[...] = hot.T.astype(jnp.bfloat16)

    def count(row, carry):
        document = lax.broadcasted_iota(jnp.int32, (block_size, seeds), 0) + row * block_size
        doc_hot = jnp.where(document == seed_doc[...], 1.0, 0.0).astype(jnp.bfloat16)
        hits = jnp.dot(doc_hot, topic_hot[...], preferred_element_type=jnp.float32)
        counts[row] = hits.astype(jnp.bfloat16)
        return carry

    lax.fori_loop(0, blocks_dev, count, 0, unroll=8)

    def step(c, carry):
        slots = [jnp.minimum(c * chunk + i, number - 1) for i in range(chunk)]
        for i, slot in enumerate(slots):

            @pl.when(c * chunk + i < number)
            def _():
                for copy in row_copies(weights, labels, held, block, sem, left[slot], slot):
                    copy.wait()

        for slot in slots:
            scale_row(held, block, extended, scales, left[slot], slot)
        return carry

    lax.fori_loop(0, lax.div(number + chunk - 1, jnp.int32(chunk)), step, 0)
    copy_out(extended, lists, toward_y(), (y_a, y_b))


def pick_body(lists, source, out, *, number):
    direction = toward_y()[number]
    for i in range(out.shape[0]):
        out[i] = source[lists[0, direction, i]]


def near(weights, extended, columns, scales, counts, row):
    topics = extended.shape[2]
    product = weighted(weights, extended, columns, row, 0, LOCAL)
    return spread_over(ALPHA * scales[row], topics) * product + SEED_WEIGHT * counts[row].astype(jnp.float32)


def near_body(columns, weights, extended, scales, counts, *rest, unroll):
    partial = rest[-1]

    def step(row, carry):
        partial[row] = near(weights, extended, columns, scales, counts, row)
        return carry

    lax.fori_loop(0, partial.shape[0], step, 0, unroll=unroll)


def arrivals(pieces, extended):
    sends = pieces[0].shape[0]
    low = extended.shape[0] - 4 * sends
    order = toward_x() + toward_y()
    i = 0
    for piece in pieces:
        extended[pl.ds(low + order[i // sends] * sends + i % sends, piece.shape[0])] = piece[...]
        i += piece.shape[0]


def finished(weights, extended, columns, scales, partial, row):
    topics = partial.shape[2]
    slots = weights.shape[1]
    product = weighted(weights, extended, columns, row, LOCAL, slots)
    return partial[row] + spread_over(ALPHA * scales[row], topics) * product


def corner_send_body(columns, lists, weights, extended_in, scales, partial, r0, r1, r2, r3, x_b, extended):
    arrivals((r1, r0, r3, r2), extended)
    send(columns, lists, weights, extended, scales, partial, toward_x()[1], x_b)


def send_body(columns, lists, weights, extended, scales, partial, out, *, number):
    send(columns, lists, weights, extended, scales, partial, (toward_x() + toward_y())[number], out)


def y_send_body(columns, lists, weights, extended, scales, partial, behind, y_a, y_b):
    for direction, out in zip(toward_y(), (y_a, y_b)):
        send(columns, lists, weights, extended, scales, partial, direction, out)


def send(columns, lists, weights, extended, scales, partial, direction, out):
    for i in range(out.shape[0]):
        row = lists[0, direction, i]
        value = finished(weights, extended, columns, scales, partial, row)
        out[i] = (spread_over(scales[row], out.shape[2]) * value).astype(jnp.bfloat16)


def rest_body(columns, weights, extended, scales, partial, following, handed, *, unroll):
    blocks_dev, _, topics = partial.shape

    def finish(row, carry):
        value = finished(weights, extended, columns, scales, partial, row)
        following[row] = (spread_over(scales[row], topics) * value).astype(jnp.bfloat16)
        return carry

    lax.fori_loop(0, blocks_dev, finish, 0, unroll=unroll)


def hand_on_body(direct, first_hop, out):
    straight = lax.axis_index("gy") % 2 == 0

    @pl.when(straight)
    def _():
        out[...] = direct[...]

    @pl.when(jnp.logical_not(straight))
    def _():
        out[...] = first_hop[...]


def last_body(
    columns, weights, extended_in, scales, partial, r0, r1, r2, r3, out, extended, block, sem, *, unroll
):
    blocks_dev = partial.shape[0]
    arrivals((r0, r1, r2, r3), extended)

    def leave(row):
        return pltpu.make_async_copy(block.at[row], out.at[row], sem.at[row])

    def step(row, carry):
        block[row] = finished(weights, extended, columns, scales, partial, row)
        leave(row).start()
        return carry

    lax.fori_loop(0, blocks_dev, step, 0, unroll=unroll)

    def settle(row, carry):
        leave(row).wait()
        return carry

    lax.fori_loop(0, blocks_dev, settle, 0)


ROUND = ((0, 1), (1, 3), (3, 2), (2, 0))
ACROSS = ((0, 2), (2, 0), (1, 3), (3, 1))
FIRST_HOP = (
    ((1, 1), (3, 1)), ((3, 1), (3, 0)), ((3, 0), (1, 0)), ((1, 0), (1, 1)),
    ((2, 1), (0, 1)), ((0, 1), (0, 0)), ((0, 0), (2, 0)), ((2, 0), (2, 1)),
)
SECOND_HOP = (
    ((0, 1), (1, 1)), ((1, 1), (3, 0)), ((3, 0), (3, 1)), ((3, 1), (2, 1)), ((2, 1), (0, 0)), ((0, 0), (0, 1)),
    ((1, 0), (2, 0)), ((2, 0), (1, 0)),
)


def neighbours(count, first):
    pairs = [p for low in range(first, count - 1, 2) for p in ((low, low + 1), (low + 1, low))]
    return pairs, [place for place in range(count) if all(place != source for source, _ in pairs)]


def permuted(value, pairs):
    inner = lax.axis_size("gy")
    return lax.ppermute(value, ("gx", "gy"), sorted((a * inner + b, c * inner + d) for (a, b), (c, d) in pairs))


def along_x(line, pairs):
    return [((source, line), (target, line)) for source, target in pairs]


def along_y(line, pairs):
    return [((line, source), (line, target)) for source, target in pairs]


def x_swap(value, first):
    outer, inner = lax.axis_size("gx"), lax.axis_size("gy")
    pairs, alone = neighbours(outer, first)
    moves = [move for line in range(inner) for move in along_x(line, pairs)]
    moves += [move for place in alone for move in along_y(place, neighbours(inner, 0)[0])]
    return permuted(value, moves)


def by_corner():
    return lax.axis_size("gx") == 4 and lax.axis_size("gy") % 2 == 0


def hop(value, moves):
    lines = range(0, lax.axis_size("gy"), 2)
    return permuted(value, [((a, low + p), (c, low + q)) for low in lines for (a, p), (c, q) in moves])


def y_swap(value, first, idle=()):
    outer, inner = lax.axis_size("gx"), lax.axis_size("gy")
    pairs, alone = neighbours(inner, first)
    moves = [move for line in range(outer) for move in along_y(line, pairs)]
    if outer != 4:
        idle = neighbours(outer, 0)[0]
    return permuted(value, moves + [move for place in alone for move in along_x(place, idle)])


def local(labels, weights, column_index, send_index, seed_doc, seed_topic):
    blocks_dev, slots, block_size, _ = weights.shape
    documents = blocks_dev * block_size
    topics = labels.shape[1]
    sends = send_index.shape[2]
    seeds = seed_doc.shape[0]
    labels = unmoved(labels.reshape(blocks_dev, block_size, topics))
    weights = unmoved(weights)
    send_index = unmoved(send_index)
    seed_doc = seed_doc.reshape(1, seeds)
    seed_topic = seed_topic.reshape(1, seeds)
    whole = VMEM((sends, block_size, topics), jnp.bfloat16)
    held_shape = VMEM(weights.shape, jnp.bfloat16)
    extended_shape = VMEM((blocks_dev + 4 * sends, block_size, topics), jnp.bfloat16)
    scale_shape = VMEM((blocks_dev, block_size, block_size), jnp.float32)
    count_shape = VMEM((blocks_dev, block_size, topics), jnp.bfloat16)
    partial_shape = VMEM((blocks_dev, block_size, topics), jnp.float32)

    x_a, x_b, held, extended, scales, columns, lists = call(
        first_send_body,
        (whole, whole, held_shape, extended_shape, scale_shape)
        + (pltpu.SMEM((slots, blocks_dev), jnp.int32), pltpu.SMEM(send_index.shape, jnp.int32)),
        (IN_VMEM,) * 5 + (IN_SMEM,) * 2,
        (ANYWHERE,) * 4,
        (
            pltpu.VMEM((2 * sends + EARLY, block_size, topics), jnp.float32),
            pltpu.SMEM((blocks_dev,), jnp.int32),
            pltpu.SMEM((2 * sends,), jnp.int32),
            pltpu.SemaphoreType.DMA((2 * sends + EARLY, 2)),
            pltpu.SemaphoreType.DMA((2,)),
        ),
    )(unmoved(column_index.T), send_index, weights, labels)
    x_b = x_swap(x_b, 1)
    x_a = x_swap(x_a, 0)
    columns, lists = tabled(columns), tabled(lists)

    held, extended, scales, counts, y_a, y_b = call(
        functools.partial(degree_body, chunk=4),
        (held_shape, extended_shape, scale_shape, count_shape, whole, whole),
        (IN_VMEM,) * 6,
        (IN_SMEM,) + (IN_VMEM,) * 2 + (ANYWHERE,) * 2 + (IN_VMEM,) * 3,
        (
            pltpu.VMEM((blocks_dev, block_size, topics), jnp.float32),
            pltpu.VMEM((seeds, topics), jnp.bfloat16),
            pltpu.SMEM((blocks_dev,), jnp.int32),
            pltpu.SMEM((blocks_dev,), jnp.int32),
            pltpu.SemaphoreType.DMA((blocks_dev, 2)),
        ),
        aliases={5: 0, 6: 1, 7: 2},
    )(lists, seed_doc, seed_topic, weights, labels, pinned(held), pinned(extended), pinned(scales))
    y_a, y_b = y_swap(y_a, 0), y_swap(y_b, 1, ROUND)
    held, scales, counts = pinned(held), pinned(scales), pinned(counts)

    def started(extended, *reused):
        return call(
            functools.partial(near_body, unroll=16),
            partial_shape,
            IN_VMEM,
            (IN_SMEM,) + (IN_VMEM,) * (4 + len(reused)),
            aliases={4 + len(reused): 0} if reused else {},
        )(columns, held, pinned(extended), scales, counts, *reused)

    partial = started(extended)
    x_b, extended = call(
        corner_send_body,
        (whole, extended_shape),
        (IN_VMEM,) * 2,
        (IN_SMEM,) * 2 + (IN_VMEM,) * 8,
        aliases={3: 1},
    )(columns, lists, held, pinned(extended), scales, pinned(partial), *map(pinned, (x_b, x_a, y_b, y_a)))
    x_a = call(functools.partial(send_body, number=0), whole, IN_VMEM, (IN_SMEM,) * 2 + (IN_VMEM,) * 4)(
        columns, lists, held, pinned(extended), scales, pinned(partial)
    )
    y_a, y_b = call(y_send_body, (whole, whole), (IN_VMEM,) * 2, (IN_SMEM,) * 2 + (IN_VMEM,) * 5)(
        columns, lists, held, pinned(extended), scales, pinned(partial), pinned(x_a)
    )
    x_a = x_swap(x_a, 0)
    if by_corner():
        first_hop = hop(x_b, FIRST_HOP)
        x_b = call(hand_on_body, whole, IN_VMEM, (IN_VMEM,) * 2)(*map(pinned, (x_b, first_hop)))
        x_b = hop(x_b, SECOND_HOP)
    else:
        x_b = x_swap(x_b, 1)
    y_a, y_b = y_swap(y_a, 0), y_swap(y_b, 1)

    following, partial = call(
        functools.partial(rest_body, unroll=16),
        (extended_shape, partial_shape),
        (IN_VMEM,) * 2,
        (IN_SMEM,) + (IN_VMEM,) * 4,
        aliases={4: 1},
    )(columns, held, pinned(extended), scales, pinned(partial))
    partial = started(following, pinned(extended), pinned(partial))

    out, _ = call(
        functools.partial(last_body, unroll=32),
        (jax.ShapeDtypeStruct((blocks_dev, block_size, topics), jnp.float32), extended_shape),
        (ANYWHERE, IN_VMEM),
        (IN_SMEM,) + (IN_VMEM,) * 8,
        (
            pltpu.VMEM((blocks_dev, block_size, topics), jnp.float32),
            pltpu.SemaphoreType.DMA((blocks_dev,)),
        ),
        aliases={2: 1},
    )(columns, held, pinned(following), scales, pinned(partial), *map(pinned, (x_a, x_b, y_a, y_b)))
    return out.reshape(documents, topics)


def solution(mesh):
    in_specs = (
        P(("gx", "gy"), None),
        P(("gx", "gy"), None, None, None),
        P(("gx", "gy"), None),
        P(("gx", "gy"), None, None),
        P(("gx", "gy")),
        P(("gx", "gy")),
    )
    out_specs = P(("gx", "gy"), None)
    return jax.shard_map(local, mesh=mesh, in_specs=in_specs, out_specs=out_specs, check_vma=False)
```
